128 devices in a mesh: owner: 32 (over z, y, core), split: 4 (over x).
Axes of the slice: x: 4, y: 4, z: 4, core: 2. Of those that a mesh axis runs over, the one named last changes fastest.
Arguments:
- emb: bfloat16 [16384, 1024], P(('owner', 'split')), may hold values from -130 to 130
- cluster: int32 [16384], P(('owner', 'split')), may hold values from 0 to 63, as said below
- owner_of: int32 [64], replicated, may hold values from 0 to 31, as said below
Outputs:
- best_cosine: float32 [16384], P(('owner', 'split'))
The draws below stay inside these ranges and needn't reach their ends.
Inputs may be any that keep to these rules, and one draw needn't show every extreme that they name: Every cluster holds at least two rows. Together with owner_of: the rows of one device whose cluster is placed on one owner number at most 8, and on every device exactly 8 for some owner. `owner_of`: each owner holds exactly 2 clusters.
All inputs are finite; a program needn't handle non-finite values.
Results may differ from the reference program's by a relative error of at most 0.00053.
Values may be sent and summed in bfloat16 or wider, within the bound.
A program may use at most 64 MiB of HBM per device.

```python
import math
import jax
import jax.numpy as jnp
from jax import lax

D = 1024
ROW_DEV = 128
CLU_OWN = 2
CAP = 8
CLUSTERS = 64
ROWS = 16384
N_OWNER = 32
N_SPLIT = 4


def cluster_plan(key):
    plan_key = jax.random.fold_in(key, 11)
    key_perm, key_shift, key_rows = jax.random.split(plan_key, 3)
    owners_total = CLUSTERS // CLU_OWN
    devices = ROWS // ROW_DEV
    placed = jax.random.permutation(key_perm, CLUSTERS).astype(jnp.int32)
    owner_table = placed // CLU_OWN
    inverse = jnp.argsort(placed).astype(jnp.int32)
    offset = jax.random.randint(key_shift, (), 0, owners_total, dtype=jnp.int32)
    slot_count = owners_total * CAP
    slot_owner = jnp.arange(slot_count, dtype=jnp.int32) // CAP
    position = jnp.arange(ROW_DEV, dtype=jnp.int32)

    def one_device(dev_key, device):
        key_a, key_b, key_c, key_d = jax.random.split(dev_key, 4)
        full_owner = (device + offset) % owners_total
        order = jax.random.permutation(key_a, slot_count).astype(jnp.int32)
        ranking = jnp.where(slot_owner == full_owner, 0, slot_count) + order
        chosen = jnp.argsort(ranking)[:ROW_DEV].astype(jnp.int32)
        row_owner = slot_owner[chosen]
        first = jax.random.randint(key_b, (ROW_DEV,), 0, CLU_OWN, dtype=jnp.int32)
        second = jax.random.randint(key_c, (ROW_DEV,), 0, CLU_OWN, dtype=jnp.int32)
        skewed = first * second // CLU_OWN
        local = jnp.where(position < CAP, position % CLU_OWN, skewed)
        labels = inverse[row_owner * CLU_OWN + local]
        shuffle = jax.random.permutation(key_d, ROW_DEV).astype(jnp.int32)
        return labels[shuffle]
    dev_keys = jax.random.split(key_rows, devices)
    labels = jax.vmap(one_device)(dev_keys, jnp.arange(devices, dtype=jnp.int32))
    return (labels.reshape(ROWS).astype(jnp.int32), owner_table.astype(jnp.int32))


def draw_cluster(key, part):
    return cluster_plan(key)[0]


def draw_owner_of(key, part):
    return cluster_plan(key)[1]


def draw_emb(key, part):
    labels = cluster_plan(key)[0]
    key = jax.random.fold_in(key, 5)
    key_noise, key_center, key_weight, key_scale = jax.random.split(key, 4)
    centers = jnp.clip(jax.random.normal(key_center, (CLUSTERS, D), jnp.float32), -5.0, 5.0)
    weight = jax.random.uniform(key_weight, (CLUSTERS,), jnp.float32, 0.0, 1.5)
    scales = jnp.exp(jax.random.uniform(key_scale, (ROWS, 1), jnp.float32, 0.0, math.log(10.0)))
    noise = jnp.clip(jax.random.normal(key_noise, (ROWS, D), jnp.float32), -5.0, 5.0)
    values = scales * (noise + weight[labels][:, None] * centers[labels])
    return values.astype(jnp.bfloat16)


def setup_inputs(seed: int = 0) -> dict:
    key_list = jax.random.split(jax.random.key(seed), 4)
    return {
        "emb": draw_emb(jax.random.fold_in(key_list[3], 71), 0),
        "cluster": draw_cluster(jax.random.fold_in(key_list[3], 71), 0),
        "owner_of": draw_owner_of(jax.random.fold_in(key_list[3], 71), 0),
    }


def reference(emb, cluster, owner_of):
    group = CAP * N_OWNER * N_SPLIT
    values = emb.astype(jnp.float32)
    unit = (values * lax.rsqrt(lax.optimization_barrier(jnp.sum(values * values, 1, keepdims=True)) + 1e-06)).astype(jnp.bfloat16)
    row_owner = owner_of[cluster].astype(jnp.int32)
    owner_hot = (row_owner[:, None] == jnp.arange(N_OWNER, dtype=jnp.int32)[None, :]).astype(jnp.int32)
    rank = lax.optimization_barrier(jnp.sum(jnp.cumsum(owner_hot, 0) * owner_hot, 1)) - 1
    slot = row_owner * group + rank
    table = jnp.full((N_OWNER * group,), ROWS, jnp.int32).at[slot].set(jnp.arange(ROWS, dtype=jnp.int32))
    table = table.reshape(N_OWNER, group)
    not_self = jnp.logical_not(jnp.eye(group, dtype=bool))

    def one_owner(row_ids):
        valid = row_ids < ROWS
        picked = jnp.minimum(row_ids, ROWS - 1)
        members = unit[picked].astype(jnp.float32)
        labels = jnp.where(valid, cluster[picked], -1)
        scores = jnp.dot(members, members.T, precision=lax.Precision.HIGHEST)
        same = (labels[:, None] == labels[None, :]) & (labels[None, :] >= 0) & not_self
        return lax.optimization_barrier(jnp.max(jnp.where(same, scores, jnp.float32(-2.0)), 1))
    best = lax.map(one_owner, table)
    result = jnp.zeros((ROWS,), jnp.float32).at[table.reshape(-1)].set(best.reshape(-1), mode='drop')
    return result
```

```python
import functools

import jax
import jax.numpy as jnp
from jax import lax
from jax.experimental import pallas as pl
from jax.experimental.pallas import tpu as pltpu
from jax.sharding import PartitionSpec as P

MESH = pl.DeviceIdType.MESH
OWNERS = 32
SPLITS = 4
CAP = 8
WIDTH = 1024
HALF = WIDTH // 2
ROWS = 128
CLUSTERS = 64
GROUPS = 4
GROUP_ROWS = 256
STEPS_PER_GROUP = OWNERS // GROUPS
MULT = 1
INV = pow(MULT, -1, 32)
STAGES = 9


def place_of(owner):
    return ((owner // 2) % 4 + owner // 8 + 2 * (owner % 2)) % SPLITS


def kernel(
    emb_ref, clu_ref, own_ref, out_ref,
    send, lab_send, recv, lab_recv, held, best, ret_recv,
    send_sem, lab_send_sem, ret_send_sem, recv_sem, lab_sem, ret_sem,
):
    me = lax.axis_index("owner")
    split = lax.axis_index("split")
    is_owner = place_of(me) == split
    barrier = pltpu.get_barrier_semaphore()

    @pl.when(is_owner)
    def _():
        def greet(p, c):
            pl.semaphore_signal(
                barrier, inc=1, device_id=((me + p // SPLITS) % OWNERS, (split + p) % SPLITS),
                device_id_type=MESH,
            )
            return c
        lax.fori_loop(1, OWNERS * SPLITS, greet, 0)

    cluster = clu_ref[...]
    hot = (lax.broadcasted_iota(jnp.int32, (CLUSTERS, ROWS), 0) == cluster).astype(jnp.bfloat16)
    table = (lax.broadcasted_iota(jnp.int32, (OWNERS, CLUSTERS), 0) == own_ref[...]).astype(jnp.bfloat16)
    owner_hot = jnp.dot(table, hot, preferred_element_type=jnp.float32)
    before = (
        lax.broadcasted_iota(jnp.int32, (ROWS, ROWS), 0) < lax.broadcasted_iota(jnp.int32, (ROWS, ROWS), 1)
    ).astype(jnp.bfloat16)
    count = jnp.dot(owner_hot.astype(jnp.bfloat16), before, preferred_element_type=jnp.float32)
    rank = jnp.sum(owner_hot * count, 0, keepdims=True).astype(jnp.int32)
    owner_id = lax.broadcasted_iota(jnp.int32, (OWNERS, ROWS), 0)
    step_id = ((owner_id - me + OWNERS) * INV) & (OWNERS - 1)
    step = jnp.sum(owner_hot * step_id.astype(jnp.float32), 0, keepdims=True).astype(jnp.int32)
    lane = ((step & 3) * SPLITS + split) * CAP + rank
    lane_hot = lax.broadcasted_iota(jnp.int32, (ROWS, ROWS), 0) == lane
    step_hot = lax.broadcasted_iota(jnp.int32, (OWNERS, ROWS), 0) == step
    step_labels = jnp.where(step_hot, (cluster + 1).astype(jnp.float32), 0.0).astype(jnp.bfloat16)
    lab_send[...] = lax.dot_general(
        step_labels, lane_hot.astype(jnp.bfloat16), (((1,), (1,)), ((), ())),
        preferred_element_type=jnp.float32,
    )
    values = emb_ref[...].astype(jnp.float32)
    unit = (values * lax.rsqrt(jnp.sum(values * values, 1, keepdims=True) + 1e-06)).astype(jnp.bfloat16)
    pick = (
        lax.broadcasted_iota(jnp.int32, (OWNERS * CAP, ROWS), 0) == step * CAP + rank
    ).astype(jnp.bfloat16)
    for h in range(2):
        rows = jnp.dot(pick, unit[:, h * HALF:(h + 1) * HALF], preferred_element_type=jnp.float32)
        if h == 0:
            low = rows.reshape(OWNERS, CAP, HALF)
        else:
            send[...] = jnp.concatenate([low, rows.reshape(OWNERS, CAP, HALF)], 1).astype(jnp.bfloat16)

    @pl.when(is_owner)
    def _():
        pl.semaphore_wait(barrier, OWNERS - 1)

    @pl.when(jnp.logical_not(is_owner))
    def _():
        pl.semaphore_wait(barrier, OWNERS)

    if STAGES >= 2:
        def post(t, c):
            to = (me + MULT * t) % OWNERS
            there = place_of(to)
            p = t * SPLITS + split
            remote = jnp.logical_not((to == me) & (there == split))

            @pl.when(remote)
            def _():
                pltpu.make_async_remote_copy(
                    src_ref=lab_send.at[pl.ds(t, 1)], dst_ref=lab_recv.at[pl.ds(p, 1)],
                    send_sem=lab_send_sem, recv_sem=lab_sem,
                    device_id=(to, there), device_id_type=MESH,
                ).start()
                pltpu.make_async_remote_copy(
                    src_ref=send.at[t], dst_ref=recv.at[p],
                    send_sem=send_sem, recv_sem=recv_sem.at[t // STEPS_PER_GROUP],
                    device_id=(to, there), device_id_type=MESH,
                ).start()
            return c
        lax.fori_loop(0, OWNERS, post, 0)

    @pl.when(is_owner)
    def _():
        if STAGES >= 2:
            recv[split] = send[0]
            lab_recv[pl.ds(split, 1)] = lab_send[0:1]
            per = STEPS_PER_GROUP * SPLITS
            pltpu.make_async_copy(lab_recv.at[pl.ds(1, 127)], lab_recv.at[pl.ds(1, 127)], lab_sem).wait()
            labels = jnp.sum(lab_recv[...].reshape(8, 16, 128), 1)
            eye = (
                lax.broadcasted_iota(jnp.int32, (ROWS, ROWS), 0) == lax.broadcasted_iota(jnp.int32, (ROWS, ROWS), 1)
            )
            columns = lax.dot_general(
                eye.astype(jnp.bfloat16), labels.astype(jnp.bfloat16), (((1,), (1,)), ((), ())),
                preferred_element_type=jnp.float32,
            )
        if STAGES < 4:
            best[...] = jnp.zeros_like(best)
        if STAGES >= 2:
            tops = [None] * 8
            for g in range(GROUPS):
                if g == 0:
                    part = recv.at[pl.ds(0, per - 1)]
                else:
                    part = recv.at[pl.ds(g * per, per)]
                pltpu.make_async_copy(part, part, recv_sem.at[g]).wait()
                if STAGES >= 4:
                    got = recv[g * per:(g + 1) * per].astype(jnp.float32)
                    held[g * GROUP_ROWS:(g + 1) * GROUP_ROWS, :HALF] = (
                        got[:, :CAP].reshape(GROUP_ROWS, HALF).astype(jnp.bfloat16)
                    )
                    held[g * GROUP_ROWS:(g + 1) * GROUP_ROWS, HALF:] = (
                        got[:, CAP:].reshape(GROUP_ROWS, HALF).astype(jnp.bfloat16)
                    )
                    for a in range(g + 1):
                        for b in ([g] if a == g else [g, -1]):
                            i, j = (a, g) if b == g else (g, a)
                            scores = lax.dot_general(
                                held[i * GROUP_ROWS:(i + 1) * GROUP_ROWS, :],
                                held[j * GROUP_ROWS:(j + 1) * GROUP_ROWS, :],
                                (((1,), (1,)), ((), ())), preferred_element_type=jnp.float32,
                            )
                            for u in range(2):
                                for v in range(2):
                                    bi, bj = 2 * i + u, 2 * j + v
                                    same = columns[:, bi:bi + 1] == labels[bj:bj + 1, :]
                                    if bi == bj:
                                        same = same & jnp.logical_not(eye)
                                    top = jnp.max(
                                        jnp.where(
                                            same, scores[u * 128:(u + 1) * 128, v * 128:(v + 1) * 128], -2.0
                                        ), 0, keepdims=True,
                                    )
                                    tops[bj] = top if tops[bj] is None else jnp.maximum(tops[bj], top)
            if STAGES >= 4:
                for b in range(8):
                    best[b:b + 1, :] = tops[b]
        if STAGES >= 3:
            def give(p, c):
                to = (me - MULT * (p // SPLITS) + OWNERS * MULT) % OWNERS
                there = p % SPLITS
                remote = jnp.logical_not((to == me) & (there == split))

                @pl.when(remote)
                def _():
                    pltpu.make_async_remote_copy(
                        src_ref=best.at[pl.ds(p // 16, 1)], dst_ref=ret_recv.at[pl.ds(me, 1)],
                        send_sem=ret_send_sem, recv_sem=ret_sem,
                        device_id=(to, there), device_id_type=MESH,
                    ).start()
                return c
            lax.fori_loop(0, OWNERS * SPLITS, give, 0)
            ret_recv[pl.ds(me, 1)] = best[0:1]
            pltpu.make_async_copy(
                ret_recv.at[pl.ds(0, OWNERS - 1)], ret_recv.at[pl.ds(0, OWNERS - 1)], ret_sem
            ).wait()
            pltpu.make_async_copy(lab_recv.at[pl.ds(0, 127)], lab_recv.at[pl.ds(0, 127)], ret_send_sem).wait()
        if STAGES >= 2:
            pltpu.make_async_copy(send.at[pl.ds(0, OWNERS - 1)], send.at[pl.ds(0, OWNERS - 1)], send_sem).wait()
            pltpu.make_async_copy(
                lab_send.at[pl.ds(0, OWNERS - 1)], lab_send.at[pl.ds(0, OWNERS - 1)], lab_send_sem
            ).wait()

    @pl.when(jnp.logical_not(is_owner))
    def _():
        if STAGES >= 3:
            pltpu.make_async_copy(ret_recv, ret_recv, ret_sem).wait()
        if STAGES >= 2:
            pltpu.make_async_copy(send, send, send_sem).wait()
            pltpu.make_async_copy(lab_send, lab_send, lab_send_sem).wait()

    if STAGES >= 3:
        spread = lax.dot_general(
            ret_recv[...], owner_hot, (((0,), (0,)), ((), ())),
            precision=lax.Precision.HIGHEST, preferred_element_type=jnp.float32,
        )
        out_ref[...] = jnp.sum(jnp.where(lane_hot, spread, 0.0), 0, keepdims=True)
    else:
        out_ref[...] = jnp.sum(jnp.where(lane_hot, 1.0, 0.0), 0, keepdims=True)


def on_device(emb, cluster, owner_of):
    vmem = pl.BlockSpec(memory_space=pltpu.VMEM)
    best = pl.pallas_call(
        kernel,
        out_shape=jax.ShapeDtypeStruct((1, ROWS), jnp.float32),
        in_specs=[vmem] * 3,
        out_specs=vmem,
        scratch_shapes=[
            pltpu.VMEM((OWNERS, 2 * CAP, HALF), jnp.bfloat16),
            pltpu.VMEM((OWNERS, 128), jnp.float32),
            pltpu.VMEM((OWNERS * SPLITS, 2 * CAP, HALF), jnp.bfloat16),
            pltpu.VMEM((OWNERS * SPLITS, 128), jnp.float32),
            pltpu.VMEM((OWNERS * SPLITS * CAP, WIDTH), jnp.bfloat16),
            pltpu.VMEM((8, 128), jnp.float32),
            pltpu.VMEM((OWNERS, 128), jnp.float32),
            pltpu.SemaphoreType.DMA,
            pltpu.SemaphoreType.DMA,
            pltpu.SemaphoreType.DMA,
            pltpu.SemaphoreType.DMA((GROUPS,)),
            pltpu.SemaphoreType.DMA,
            pltpu.SemaphoreType.DMA,
        ],
        compiler_params=pltpu.CompilerParams(
            collective_id=0, has_side_effects=True, vmem_limit_bytes=32 * 1024 * 1024
        ),
    )(emb, cluster.reshape(1, ROWS), owner_of.reshape(1, CLUSTERS))
    return best.reshape(ROWS)


def solution(mesh):
    return jax.shard_map(
        on_device,
        mesh=mesh,
        in_specs=(P(("owner", "split"), None), P(("owner", "split")), P()),
        out_specs=P(("owner", "split")),
        check_vma=False,
    )
```

```python
import jax
import jax.numpy as jnp
from jax import lax
from jax.experimental import pallas as pl
from jax.experimental.pallas import tpu as pltpu
from jax.sharding import PartitionSpec as P

MESH = pl.DeviceIdType.MESH
OWNERS = 32
SPLITS = 4
CAP = 8
WIDTH = 1024
HALF = WIDTH // 2
ROWS = 128
CLUSTERS = 64
DEVICES = OWNERS * SPLITS
GROUPS = 4
PER = DEVICES // GROUPS
GROUP_ROWS = PER * CAP
CORE = 1
VL = 24
STAGES = 9
MULT = 1
ORDER = 1
FLIP = 0
SPIN_X = 1
SPIN_M = 1
UNROLL = 4


def home_of(o):
    return lax.div(o, 4) * 2 + CORE, lax.rem(o, 4)


def owner_at(me, split):
    return (lax.rem(me, 2) == CORE) & (me < 16), lax.rem(lax.div(me, 2), 8) * 4 + split


def spot_of(z, y, core):
    if ORDER == 0:
        return z * 32 + core * 16 + y * 4
    return core * 64 + z * 16 + y * 4


def iota(shape, dim):
    return lax.broadcasted_iota(jnp.int32, shape, dim)


def wait_bytes(ref, sem):
    pltpu.make_async_copy(ref, ref, sem).wait()


def kernel(
    emb_hbm, clu_hbm, own_hbm, out_ref,
    emb_ref, clu_ref, own_ref, send, lab_send, recv, lab_recv, held, best, ret_recv,
    load_sem, send_sem, lab_send_sem, ret_send_sem, recv_sem, lab_sem, ret_sem,
):
    me = lax.axis_index("owner")
    split = lax.axis_index("split")
    is_owner, mine = owner_at(me, split)
    z, y, core = lax.div(me, 8), lax.rem(lax.div(me, 2), 4), lax.rem(me, 2)
    here = spot_of(z, y, core) + split
    loads = [
        pltpu.make_async_copy(src, dst, load_sem.at[i])
        for i, (src, dst) in enumerate(((clu_hbm, clu_ref), (own_hbm, own_ref), (emb_hbm, emb_ref)))
    ]
    for load in loads:
        load.start()
    barrier = pltpu.get_barrier_semaphore()

    @pl.when(is_owner)
    def _():
        for q in range(1, SPLITS):
            pl.semaphore_signal(
                barrier, inc=1, device_id=(me, lax.rem(split + q, SPLITS)), device_id_type=MESH
            )

        def greet(t, c):
            to = lax.rem(me + OWNERS - t, OWNERS)
            for q in range(SPLITS):
                pl.semaphore_signal(barrier, inc=1, device_id=(to, q), device_id_type=MESH)
            return c
        lax.fori_loop(1, OWNERS, greet, 0, unroll=UNROLL)

    loads[0].wait()
    loads[1].wait()
    cluster = clu_ref[...]
    hot = (iota((CLUSTERS, ROWS), 0) == cluster).astype(jnp.bfloat16)
    table = (iota((OWNERS, CLUSTERS), 0) == own_ref[...]).astype(jnp.bfloat16)
    owner_hot = jnp.dot(table, hot, preferred_element_type=jnp.float32)
    before = (iota((ROWS, ROWS), 0) < iota((ROWS, ROWS), 1)).astype(jnp.bfloat16)
    count = jnp.dot(owner_hot.astype(jnp.bfloat16), before, preferred_element_type=jnp.float32)
    slot = jnp.sum(
        owner_hot * (count + CAP * iota((OWNERS, ROWS), 0).astype(jnp.float32)), 0, keepdims=True
    ).astype(jnp.int32)
    rank = slot & (CAP - 1)
    lane_hot = iota((ROWS, ROWS), 0) == lax.rem(here, 16) * CAP + rank
    labels = (owner_hot * (cluster + 1).astype(jnp.float32)).astype(jnp.bfloat16)
    lab_send[...] = lax.dot_general(
        labels, lane_hot.astype(jnp.bfloat16), (((1,), (1,)), ((), ())),
        preferred_element_type=jnp.float32,
    )
    loads[2].wait()
    values = emb_ref[...].astype(jnp.float32)
    unit = (values * lax.rsqrt(jnp.sum(values * values, 1, keepdims=True) + 1e-06)).astype(jnp.bfloat16)
    pick = (iota((OWNERS * CAP, ROWS), 0) == slot).astype(jnp.bfloat16)
    parts = [
        jnp.dot(pick, unit[:, h * HALF:(h + 1) * HALF], preferred_element_type=jnp.float32).reshape(
            OWNERS, CAP, HALF
        )
        for h in range(2)
    ]
    send[...] = jnp.concatenate(parts, 1).astype(jnp.bfloat16)

    @pl.when(is_owner)
    def _():
        pl.semaphore_wait(barrier, OWNERS - 1)

    @pl.when(jnp.logical_not(is_owner))
    def _():
        pl.semaphore_wait(barrier, OWNERS)

    group = lax.div(here, PER)

    def send_step(o):
        there = home_of(o)
        pltpu.make_async_remote_copy(
            src_ref=lab_send.at[pl.ds(o, 1)], dst_ref=lab_recv.at[pl.ds(here, 1)],
            send_sem=lab_send_sem, recv_sem=lab_sem, device_id=there, device_id_type=MESH,
        ).start()
        pltpu.make_async_remote_copy(
            src_ref=send.at[o], dst_ref=recv.at[here],
            send_sem=send_sem, recv_sem=recv_sem.at[group], device_id=there, device_id_type=MESH,
        ).start()

    first = lax.rem(SPIN_X * split + SPIN_M * me, OWNERS)

    def post(t, c):
        o = lax.rem(first + MULT * t, OWNERS)

        @pl.when(jnp.logical_not(is_owner & (o == mine)))
        def _():
            send_step(o)
        return c
    if STAGES >= 2:
        lax.fori_loop(0, OWNERS, post, 0, unroll=UNROLL)

    @pl.when(is_owner)
    def _():
        if STAGES >= 2:
            recv[here] = send[mine]
            lab_recv[pl.ds(here, 1)] = lab_send[pl.ds(mine, 1)]
            wait_bytes(lab_recv.at[pl.ds(0, DEVICES - 1)], lab_sem)
            labels = jnp.sum(lab_recv[...].reshape(8, 16, 128), 1)
            eye = iota((ROWS, ROWS), 0) == iota((ROWS, ROWS), 1)
            columns = lax.dot_general(
                eye.astype(jnp.bfloat16), labels.astype(jnp.bfloat16), (((1,), (1,)), ((), ())),
                preferred_element_type=jnp.float32,
            )
            tops, wides = [None] * 8, [None] * 6
            for g in range(GROUPS):
                @pl.when(group == g)
                def _():
                    wait_bytes(recv.at[pl.ds(0, PER - 1)], recv_sem.at[g])

                @pl.when(group != g)
                def _():
                    wait_bytes(recv.at[pl.ds(0, PER)], recv_sem.at[g])
                if STAGES < 4:
                    continue
                got = recv[g * PER:(g + 1) * PER].astype(jnp.float32)
                for h in range(2):
                    held[g * GROUP_ROWS:(g + 1) * GROUP_ROWS, h * HALF:(h + 1) * HALF] = (
                        got[:, h * CAP:(h + 1) * CAP].reshape(GROUP_ROWS, HALF).astype(jnp.bfloat16)
                    )
                seen = (g + 1) * GROUP_ROWS
                scores = lax.dot_general(
                    held[0:seen, :], held[g * GROUP_ROWS:seen, :], (((1,), (1,)), ((), ())),
                    preferred_element_type=jnp.float32,
                )
                for bi in range(2 * g + 2):
                    wide = None
                    for v in range(2):
                        bj = 2 * g + v
                        same = columns[:, bi:bi + 1] == labels[bj:bj + 1, :]
                        if bi == bj:
                            same = same & jnp.logical_not(eye)
                        kept = jnp.where(same, scores[bi * 128:(bi + 1) * 128, v * 128:(v + 1) * 128], -2.0)
                        top = jnp.max(kept, 0, keepdims=True)
                        tops[bj] = top if tops[bj] is None else jnp.maximum(tops[bj], top)
                        wide = kept if wide is None else jnp.maximum(wide, kept)
                    if bi < 2 * g:
                        wides[bi] = wide if wides[bi] is None else jnp.maximum(wides[bi], wide)
            if STAGES >= 4:
                for b in range(6):
                    if FLIP == 0:
                        top = jnp.max(jnp.transpose(wides[b]), 0, keepdims=True)
                    else:
                        col = jnp.max(wides[b], 1, keepdims=True)
                        top = jnp.max(jnp.where(eye, col, -2.0), 0, keepdims=True)
                    tops[b] = jnp.maximum(tops[b], top)
            for b in range(8):
                best[b:b + 1, :] = tops[b] if STAGES >= 4 else jnp.zeros((1, 128), jnp.float32)
        if STAGES >= 3:
            def give(m, c):
                for q in range(SPLITS):
                    @pl.when(jnp.logical_not((m == me) & (q == split)))
                    def _():
                        pltpu.make_async_remote_copy(
                            src_ref=best.at[pl.ds(lax.div(spot_of(lax.div(m, 8), lax.rem(lax.div(m, 2), 4), lax.rem(m, 2)), 16), 1)], dst_ref=ret_recv.at[pl.ds(mine, 1)],
                            send_sem=ret_send_sem, recv_sem=ret_sem,
                            device_id=(m, q), device_id_type=MESH,
                        ).start()
                return c
            lax.fori_loop(0, OWNERS, give, 0, unroll=UNROLL)
            ret_recv[pl.ds(mine, 1)] = best[pl.ds(lax.div(here, 16), 1)]
            wait_bytes(ret_recv.at[pl.ds(0, OWNERS - 1)], ret_sem)

    if STAGES >= 3:
        @pl.when(jnp.logical_not(is_owner))
        def _():
            wait_bytes(ret_recv, ret_sem)
        rest = ret_recv[...]
        terms = []
        for _ in range(3):
            terms.append(rest.astype(jnp.bfloat16))
            rest = rest - terms[-1].astype(jnp.float32)
        spread = lax.dot_general(
            jnp.concatenate(terms, 0), jnp.concatenate([owner_hot.astype(jnp.bfloat16)] * 3, 0),
            (((0,), (0,)), ((), ())), preferred_element_type=jnp.float32,
        )
        out_ref[...] = jnp.sum(jnp.where(lane_hot, spread, 0.0), 0, keepdims=True)
    else:
        out_ref[...] = jnp.sum(jnp.where(lane_hot, 1.0, 0.0), 0, keepdims=True)

    @pl.when(is_owner)
    def _():
        wait_bytes(send.at[pl.ds(0, OWNERS - 1)], send_sem)
        wait_bytes(lab_send.at[pl.ds(0, OWNERS - 1)], lab_send_sem)
        if STAGES >= 3:
            wait_bytes(lab_recv.at[pl.ds(0, DEVICES - 1)], ret_send_sem)

    @pl.when(jnp.logical_not(is_owner))
    def _():
        wait_bytes(send, send_sem)
        wait_bytes(lab_send, lab_send_sem)


def on_device(emb, cluster, owner_of):
    best = pl.pallas_call(
        kernel,
        out_shape=jax.ShapeDtypeStruct((1, ROWS), jnp.float32),
        in_specs=[pl.BlockSpec(memory_space=pltpu.HBM)] * 3,
        out_specs=pl.BlockSpec(memory_space=pltpu.VMEM),
        scratch_shapes=[
            pltpu.VMEM((ROWS, WIDTH), jnp.bfloat16),
            pltpu.VMEM((1, ROWS), jnp.int32),
            pltpu.VMEM((1, CLUSTERS), jnp.int32),
            pltpu.VMEM((OWNERS, 2 * CAP, HALF), jnp.bfloat16),
            pltpu.VMEM((OWNERS, 128), jnp.float32),
            pltpu.VMEM((DEVICES, 2 * CAP, HALF), jnp.bfloat16),
            pltpu.VMEM((DEVICES, 128), jnp.float32),
            pltpu.VMEM((DEVICES * CAP, WIDTH), jnp.bfloat16),
            pltpu.VMEM((8, 128), jnp.float32),
            pltpu.VMEM((OWNERS, 128), jnp.float32),
            pltpu.SemaphoreType.DMA((3,)),
            pltpu.SemaphoreType.DMA,
            pltpu.SemaphoreType.DMA,
            pltpu.SemaphoreType.DMA,
            pltpu.SemaphoreType.DMA((GROUPS,)),
            pltpu.SemaphoreType.DMA,
            pltpu.SemaphoreType.DMA,
        ],
        compiler_params=pltpu.CompilerParams(
            collective_id=0, has_side_effects=True, vmem_limit_bytes=VL * 1024 * 1024
        ),
    )(*[
        pltpu.with_memory_space_constraint(a, pltpu.HBM)
        for a in (emb, cluster.reshape(1, ROWS), owner_of.reshape(1, CLUSTERS))
    ])
    return best.reshape(ROWS)


def solution(mesh):
    return jax.shard_map(
        on_device,
        mesh=mesh,
        in_specs=(P(("owner", "split"), None), P(("owner", "split")), P()),
        out_specs=P(("owner", "split")),
        check_vma=False,
    )
```

```python
import jax
import jax.numpy as jnp
from jax import lax
from jax.experimental import pallas as pl
from jax.experimental.pallas import tpu as pltpu
from jax.sharding import PartitionSpec as P

MESH = pl.DeviceIdType.MESH
OWNERS = 32
SPLITS = 4
CAP = 8
WIDTH = 1024
HALF = WIDTH // 2
ROWS = 128
CLUSTERS = 64
DEVICES = OWNERS * SPLITS
GROUPS = 4
PER = DEVICES // GROUPS
GROUP_ROWS = PER * CAP
STAGES = 9
UNROLL = 4
MULT = 1
SPIN_X = 1
SPIN_M = 1


def home_of(o):
    return lax.div(o, 4) * 2 + 1, lax.rem(o, 4)


def iota(shape, dim):
    return lax.broadcasted_iota(jnp.int32, shape, dim)


def wait_bytes(ref, sem):
    pltpu.make_async_copy(ref, ref, sem).wait()


def kernel(
    emb_hbm, clu_hbm, own_hbm, out_ref,
    emb_ref, clu_ref, own_ref, send, lab_send, recv, lab_recv, held, best, ret_recv,
    load_sem, send_sem, lab_send_sem, ret_send_sem, recv_sem, lab_sem, ret_sem,
):
    me = lax.axis_index("owner")
    split = lax.axis_index("split")
    here = me * SPLITS + split
    is_owner = (lax.rem(me, 2) == 1) & (me < 16)
    mine = lax.rem(lax.div(me, 2), 8) * 4 + split
    loads = [
        pltpu.make_async_copy(src, dst, load_sem.at[i])
        for i, (src, dst) in enumerate(((clu_hbm, clu_ref), (own_hbm, own_ref), (emb_hbm, emb_ref)))
    ]
    for load in loads:
        load.start()
    barrier = pltpu.get_barrier_semaphore()

    @pl.when(is_owner)
    def _():
        def greet(t, c):
            to = OWNERS - 1 - t
            for q in range(SPLITS):
                @pl.when(jnp.logical_not((to == me) & (q == split)))
                def _():
                    pl.semaphore_signal(barrier, inc=1, device_id=(to, q), device_id_type=MESH)
            return c
        lax.fori_loop(0, OWNERS, greet, 0, unroll=UNROLL)

    loads[0].wait()
    loads[1].wait()
    cluster = clu_ref[...]
    hot = (iota((CLUSTERS, ROWS), 0) == cluster).astype(jnp.bfloat16)
    table = (iota((OWNERS, CLUSTERS), 0) == own_ref[...]).astype(jnp.bfloat16)
    owner_hot = jnp.dot(table, hot, preferred_element_type=jnp.float32)
    before = (iota((ROWS, ROWS), 0) < iota((ROWS, ROWS), 1)).astype(jnp.bfloat16)
    count = jnp.dot(owner_hot.astype(jnp.bfloat16), before, preferred_element_type=jnp.float32)
    slot = jnp.sum(
        owner_hot * (count + CAP * iota((OWNERS, ROWS), 0).astype(jnp.float32)), 0, keepdims=True
    ).astype(jnp.int32)
    lane_hot = iota((ROWS, ROWS), 0) == lax.rem(here, 16) * CAP + (slot & (CAP - 1))
    labels = (owner_hot * (cluster + 1).astype(jnp.float32)).astype(jnp.bfloat16)
    lab_send[...] = lax.dot_general(
        labels, lane_hot.astype(jnp.bfloat16), (((1,), (1,)), ((), ())),
        preferred_element_type=jnp.float32,
    )
    loads[2].wait()
    values = emb_ref[...].astype(jnp.float32)
    unit = (values * lax.rsqrt(jnp.sum(values * values, 1, keepdims=True) + 1e-06)).astype(jnp.bfloat16)
    pick = (iota((OWNERS * CAP, ROWS), 0) == slot).astype(jnp.bfloat16)
    parts = [
        jnp.dot(pick, unit[:, h * HALF:(h + 1) * HALF], preferred_element_type=jnp.float32).reshape(
            OWNERS, CAP, HALF
        )
        for h in range(2)
    ]
    send[...] = jnp.concatenate(parts, 1).astype(jnp.bfloat16)
    pl.semaphore_wait(barrier, jnp.where(is_owner, OWNERS - 1, OWNERS))
    first = lax.rem(SPIN_X * split + SPIN_M * me, OWNERS)

    def post(t, c):
        o = lax.rem(first + MULT * t, OWNERS)

        @pl.when(jnp.logical_not(is_owner & (o == mine)))
        def _():
            there = home_of(o)
            pltpu.make_async_remote_copy(
                src_ref=lab_send.at[pl.ds(o, 1)], dst_ref=lab_recv.at[pl.ds(here, 1)],
                send_sem=lab_send_sem, recv_sem=lab_sem, device_id=there, device_id_type=MESH,
            ).start()
            pltpu.make_async_remote_copy(
                src_ref=send.at[o], dst_ref=recv.at[here],
                send_sem=send_sem, recv_sem=recv_sem, device_id=there, device_id_type=MESH,
            ).start()
        return c
    if STAGES >= 2:
        lax.fori_loop(0, OWNERS, post, 0, unroll=UNROLL)

    @pl.when(is_owner)
    def _():
        if STAGES >= 2:
            recv[here] = send[mine]
            lab_recv[pl.ds(here, 1)] = lab_send[pl.ds(mine, 1)]
            wait_bytes(lab_recv.at[pl.ds(0, DEVICES - 1)], lab_sem)
            labels = jnp.sum(lab_recv[...].reshape(8, 16, 128), 1)
            eye = iota((ROWS, ROWS), 0) == iota((ROWS, ROWS), 1)
            columns = lax.dot_general(
                eye.astype(jnp.bfloat16), labels.astype(jnp.bfloat16), (((1,), (1,)), ((), ())),
                preferred_element_type=jnp.float32,
            )
            wait_bytes(recv.at[pl.ds(0, DEVICES - 1)], recv_sem)
        tops, wides = [None] * 8, [None] * 6
        if STAGES >= 4:
            got = recv[...].astype(jnp.float32)
            for h in range(2):
                held[:, h * HALF:(h + 1) * HALF] = (
                    got[:, h * CAP:(h + 1) * CAP].reshape(DEVICES * CAP, HALF).astype(jnp.bfloat16)
                )
            for g in range(GROUPS):
                seen = (g + 1) * GROUP_ROWS
                scores = lax.dot_general(
                    held[0:seen, :], held[g * GROUP_ROWS:seen, :], (((1,), (1,)), ((), ())),
                    preferred_element_type=jnp.float32,
                )
                for bi in range(2 * g + 2):
                    wide = None
                    for v in range(2):
                        bj = 2 * g + v
                        same = columns[:, bi:bi + 1] == labels[bj:bj + 1, :]
                        if bi == bj:
                            same = same & jnp.logical_not(eye)
                        kept = jnp.where(same, scores[bi * 128:(bi + 1) * 128, v * 128:(v + 1) * 128], -2.0)
                        top = jnp.max(kept, 0, keepdims=True)
                        tops[bj] = top if tops[bj] is None else jnp.maximum(tops[bj], top)
                        wide = kept if wide is None else jnp.maximum(wide, kept)
                    if bi < 2 * g:
                        wides[bi] = wide if wides[bi] is None else jnp.maximum(wides[bi], wide)
            for b in range(6):
                tops[b] = jnp.maximum(tops[b], jnp.max(jnp.transpose(wides[b]), 0, keepdims=True))
        for b in range(8):
            best[b:b + 1, :] = tops[b] if STAGES >= 4 else jnp.zeros((1, 128), jnp.float32)
        if STAGES >= 3:
            def give(m, c):
                for q in range(SPLITS):
                    @pl.when(jnp.logical_not((m == me) & (q == split)))
                    def _():
                        pltpu.make_async_remote_copy(
                            src_ref=best.at[pl.ds(lax.div(m, 4), 1)], dst_ref=ret_recv.at[pl.ds(mine, 1)],
                            send_sem=ret_send_sem, recv_sem=ret_sem,
                            device_id=(m, q), device_id_type=MESH,
                        ).start()
                return c
            lax.fori_loop(0, OWNERS, give, 0, unroll=UNROLL)
            ret_recv[pl.ds(mine, 1)] = best[pl.ds(lax.div(here, 16), 1)]
            wait_bytes(ret_recv.at[pl.ds(0, OWNERS - 1)], ret_sem)

    if STAGES >= 3:
        @pl.when(jnp.logical_not(is_owner))
        def _():
            wait_bytes(ret_recv, ret_sem)
        rest = ret_recv[...]
        terms = []
        for _ in range(3):
            terms.append(rest.astype(jnp.bfloat16))
            rest = rest - terms[-1].astype(jnp.float32)
        spread = lax.dot_general(
            jnp.concatenate(terms, 0), jnp.concatenate([owner_hot.astype(jnp.bfloat16)] * 3, 0),
            (((0,), (0,)), ((), ())), preferred_element_type=jnp.float32,
        )
        out_ref[...] = jnp.sum(jnp.where(lane_hot, spread, 0.0), 0, keepdims=True)
    else:
        out_ref[...] = jnp.sum(jnp.where(lane_hot, 1.0, 0.0), 0, keepdims=True)

    if STAGES >= 2:
        @pl.when(is_owner)
        def _():
            wait_bytes(send.at[pl.ds(0, OWNERS - 1)], send_sem)
            wait_bytes(lab_send.at[pl.ds(0, OWNERS - 1)], lab_send_sem)
            if STAGES >= 3:
                wait_bytes(lab_recv.at[pl.ds(0, DEVICES - 1)], ret_send_sem)

        @pl.when(jnp.logical_not(is_owner))
        def _():
            wait_bytes(send, send_sem)
            wait_bytes(lab_send, lab_send_sem)


def on_device(emb, cluster, owner_of):
    best = pl.pallas_call(
        kernel,
        out_shape=jax.ShapeDtypeStruct((1, ROWS), jnp.float32),
        in_specs=[pl.BlockSpec(memory_space=pltpu.HBM)] * 3,
        out_specs=pl.BlockSpec(memory_space=pltpu.VMEM),
        scratch_shapes=[
            pltpu.VMEM((ROWS, WIDTH), jnp.bfloat16),
            pltpu.VMEM((1, ROWS), jnp.int32),
            pltpu.VMEM((1, CLUSTERS), jnp.int32),
            pltpu.VMEM((OWNERS, 2 * CAP, HALF), jnp.bfloat16),
            pltpu.VMEM((OWNERS, 128), jnp.float32),
            pltpu.VMEM((DEVICES, 2 * CAP, HALF), jnp.bfloat16),
            pltpu.VMEM((DEVICES, 128), jnp.float32),
            pltpu.VMEM((DEVICES * CAP, WIDTH), jnp.bfloat16),
            pltpu.VMEM((8, 128), jnp.float32),
            pltpu.VMEM((OWNERS, 128), jnp.float32),
            pltpu.SemaphoreType.DMA((3,)),
            pltpu.SemaphoreType.DMA,
            pltpu.SemaphoreType.DMA,
            pltpu.SemaphoreType.DMA,
            pltpu.SemaphoreType.DMA,
            pltpu.SemaphoreType.DMA,
            pltpu.SemaphoreType.DMA,
        ],
        compiler_params=pltpu.CompilerParams(
            collective_id=0, has_side_effects=True, vmem_limit_bytes=24 * 1024 * 1024
        ),
    )(*[
        pltpu.with_memory_space_constraint(a, pltpu.HBM)
        for a in (emb, cluster.reshape(1, ROWS), owner_of.reshape(1, CLUSTERS))
    ])
    return best.reshape(ROWS)


def solution(mesh):
    return jax.shard_map(
        on_device,
        mesh=mesh,
        in_specs=(P(("owner", "split"), None), P(("owner", "split")), P()),
        out_specs=P(("owner", "split")),
        check_vma=False,
    )
```

```python
import jax
import jax.numpy as jnp
from jax import lax
from jax.experimental import pallas as pl
from jax.experimental.pallas import tpu as pltpu
from jax.sharding import PartitionSpec as P

MESH = pl.DeviceIdType.MESH
OWNERS = 32
SPLITS = 4
CAP = 8
WIDTH = 1024
HALF = WIDTH // 2
ROWS = 128
CLUSTERS = 64
DEVICES = OWNERS * SPLITS
GROUPS = 4
PER = DEVICES // GROUPS
GROUP_ROWS = PER * CAP
UNROLL = 4
MULT = 1
SPIN_X = 4
SPIN_M = 8


def home_of(o):
    return lax.div(o, 4) * 2 + 1, lax.rem(o, 4)


def iota(shape, dim):
    return lax.broadcasted_iota(jnp.int32, shape, dim)


def wait_bytes(ref, sem):
    pltpu.make_async_copy(ref, ref, sem).wait()


def kernel(
    emb_hbm, clu_hbm, own_hbm, out_ref,
    emb_ref, clu_ref, own_ref, send, lab_send, recv, lab_recv, held, soon, best, ret_recv,
    load_sem, send_sem, lab_send_sem, ret_send_sem, recv_sem, lab_sem, ret_sem,
):
    me = lax.axis_index("owner")
    split = lax.axis_index("split")
    z, y, core = lax.div(me, 8), lax.rem(lax.div(me, 2), 4), lax.rem(me, 2)
    here = (
        lax.div(z, 2) * 64 + lax.div(y, 2) * 32 + lax.div(split, 2) * 16
        + lax.rem(y, 2) * 8 + lax.rem(split, 2) * 4 + lax.rem(z, 2) * 2 + core
    )
    is_owner = (lax.rem(me, 2) == 1) & (me < 16)
    mine = lax.rem(lax.div(me, 2), 8) * 4 + split
    loads = [
        pltpu.make_async_copy(src, dst, load_sem.at[i])
        for i, (src, dst) in enumerate(((clu_hbm, clu_ref), (own_hbm, own_ref), (emb_hbm, emb_ref)))
    ]
    for load in loads:
        load.start()
    barrier = pltpu.get_barrier_semaphore()

    @pl.when(is_owner)
    def _():
        def greet(t, c):
            to = OWNERS - 1 - t
            for q in range(SPLITS):
                @pl.when(jnp.logical_not((to == me) & (q == split)))
                def _():
                    pl.semaphore_signal(barrier, inc=1, device_id=(to, q), device_id_type=MESH)
            return c
        lax.fori_loop(0, OWNERS, greet, 0, unroll=UNROLL)

    loads[0].wait()
    loads[1].wait()
    cluster = clu_ref[...]
    hot = (iota((CLUSTERS, ROWS), 0) == cluster).astype(jnp.bfloat16)
    table = (iota((OWNERS, CLUSTERS), 0) == own_ref[...]).astype(jnp.bfloat16)
    owner_hot = jnp.dot(table, hot, preferred_element_type=jnp.float32)
    before = (iota((ROWS, ROWS), 0) < iota((ROWS, ROWS), 1)).astype(jnp.bfloat16)
    count = jnp.dot(owner_hot.astype(jnp.bfloat16), before, preferred_element_type=jnp.float32)
    slot = jnp.sum(
        owner_hot * (count + CAP * iota((OWNERS, ROWS), 0).astype(jnp.float32)), 0, keepdims=True
    ).astype(jnp.int32)
    lane_hot = iota((ROWS, ROWS), 0) == lax.rem(here, 16) * CAP + (slot & (CAP - 1))
    labels = (owner_hot * (cluster + 1).astype(jnp.float32)).astype(jnp.bfloat16)
    lab_send[...] = lax.dot_general(
        labels, lane_hot.astype(jnp.bfloat16), (((1,), (1,)), ((), ())),
        preferred_element_type=jnp.float32,
    )
    loads[2].wait()
    values = emb_ref[...].astype(jnp.float32)
    unit = (values * lax.rsqrt(jnp.sum(values * values, 1, keepdims=True) + 1e-06)).astype(jnp.bfloat16)
    pick = (iota((OWNERS * CAP, ROWS), 0) == slot).astype(jnp.bfloat16)
    parts = [
        jnp.dot(pick, unit[:, h * HALF:(h + 1) * HALF], preferred_element_type=jnp.float32).reshape(
            OWNERS, CAP, HALF
        )
        for h in range(2)
    ]
    send[...] = jnp.concatenate(parts, 1).astype(jnp.bfloat16)
    pl.semaphore_wait(barrier, jnp.where(is_owner, OWNERS - 1, OWNERS))
    first = lax.rem(SPIN_X * split + SPIN_M * me, OWNERS)

    def post(t, c):
        o = lax.rem(first + MULT * t, OWNERS)

        @pl.when(jnp.logical_not(is_owner & (o == mine)))
        def _():
            there = home_of(o)
            pltpu.make_async_remote_copy(
                src_ref=lab_send.at[pl.ds(o, 1)], dst_ref=lab_recv.at[pl.ds(here, 1)],
                send_sem=lab_send_sem, recv_sem=lab_sem, device_id=there, device_id_type=MESH,
            ).start()
            pltpu.make_async_remote_copy(
                src_ref=send.at[o], dst_ref=recv.at[here],
                send_sem=send_sem, recv_sem=recv_sem.at[lax.div(z, 2)], device_id=there, device_id_type=MESH,
            ).start()
        return c
    lax.fori_loop(0, OWNERS, post, 0, unroll=UNROLL)

    @pl.when(is_owner)
    def _():
        recv[here] = send[mine]
        lab_recv[pl.ds(here, 1)] = lab_send[pl.ds(mine, 1)]
        wait_bytes(lab_recv.at[pl.ds(0, DEVICES - 1)], lab_sem)
        labels = jnp.sum(lab_recv[...].reshape(8, 16, 128), 1)
        eye = iota((ROWS, ROWS), 0) == iota((ROWS, ROWS), 1)
        columns = lax.dot_general(
            eye.astype(jnp.bfloat16), labels.astype(jnp.bfloat16), (((1,), (1,)), ((), ())),
            preferred_element_type=jnp.float32,
        )
        tops, wides = [None] * 8, [None] * 8

        def take(begin, end):
            got = recv[begin // CAP:end // CAP].astype(jnp.float32)
            for h in range(2):
                held[begin:end, h * HALF:(h + 1) * HALF] = (
                    got[:, h * CAP:(h + 1) * CAP].reshape(end - begin, HALF).astype(jnp.bfloat16)
                )

        def score(rows, cols):
            scores = lax.dot_general(
                held[rows[0] * 128:rows[1] * 128, :], held[cols[0] * 128:cols[1] * 128, :],
                (((1,), (1,)), ((), ())), preferred_element_type=jnp.float32,
            )
            for i in range(*rows):
                for j in range(*cols):
                    same = columns[:, i:i + 1] == labels[j:j + 1, :]
                    if i == j:
                        same = same & jnp.logical_not(eye)
                    u, v = (i - rows[0]) * 128, (j - cols[0]) * 128
                    kept = jnp.where(same, scores[u:u + 128, v:v + 128], -2.0)
                    top = jnp.max(kept, 0, keepdims=True)
                    tops[j] = top if tops[j] is None else jnp.maximum(tops[j], top)
                    if not cols[0] <= i < cols[1]:
                        wides[i] = kept if wides[i] is None else jnp.maximum(wides[i], kept)

        def close(i):
            if wides[i] is not None:
                tops[i] = jnp.maximum(tops[i], jnp.max(jnp.transpose(wides[i]), 0, keepdims=True))

        def give(src, m, x):
            @pl.when(jnp.logical_not((m == me) & (x == split)))
            def _():
                pltpu.make_async_remote_copy(
                    src_ref=src, dst_ref=ret_recv.at[pl.ds(mine, 1)],
                    send_sem=ret_send_sem, recv_sem=ret_sem, device_id=(m, x), device_id_type=MESH,
                ).start()

        wait_bytes(recv.at[pl.ds(0, DEVICES // 2 - 1)], recv_sem.at[0])
        take(0, 512)
        score((0, 2), (0, 2))
        score((0, 4), (2, 4))
        close(0)
        close(1)
        wait_bytes(recv.at[pl.ds(0, DEVICES // 2)], recv_sem.at[1])
        take(512, 1024)
        score((4, 8), (0, 2))
        for b in range(2):
            soon[b:b + 1, :] = tops[b]
        for m in (1, 0, 9, 8, 3, 2, 11, 10):
            for x in range(SPLITS):
                give(soon.at[pl.ds(x // 2, 1)], m, x)
        score((4, 8), (2, 4))
        score((4, 6), (4, 6))
        score((4, 8), (6, 8))
        for b in range(4, 6):
            close(b)
        for b in range(6, 8):
            close(b)
        for b in range(8):
            best[b:b + 1, :] = tops[b]

        def give_row(m, c):
            z_to, y_to = lax.div(m, 8), lax.rem(lax.div(m, 2), 4)
            block = lax.div(z_to, 2) * 4 + lax.div(y_to, 2) * 2

            @pl.when(block != 0)
            def _():
                for x in range(SPLITS):
                    give(best.at[pl.ds(block + x // 2, 1)], m, x)
            return c
        lax.fori_loop(0, OWNERS, give_row, 0)
        ret_recv[pl.ds(mine, 1)] = best[pl.ds(lax.div(here, 16), 1)]
        wait_bytes(ret_recv.at[pl.ds(0, OWNERS - 1)], ret_sem)

    @pl.when(jnp.logical_not(is_owner))
    def _():
        wait_bytes(ret_recv, ret_sem)
    rest = ret_recv[...]
    terms = []
    for _ in range(3):
        terms.append(rest.astype(jnp.bfloat16))
        rest = rest - terms[-1].astype(jnp.float32)
    spread = lax.dot_general(
        jnp.concatenate(terms, 0), jnp.concatenate([owner_hot.astype(jnp.bfloat16)] * 3, 0),
        (((0,), (0,)), ((), ())), preferred_element_type=jnp.float32,
    )
    out_ref[...] = jnp.sum(jnp.where(lane_hot, spread, 0.0), 0, keepdims=True)
    @pl.when(is_owner)
    def _():
        wait_bytes(send.at[pl.ds(0, OWNERS - 1)], send_sem)
        wait_bytes(lab_send.at[pl.ds(0, OWNERS - 1)], lab_send_sem)
        wait_bytes(lab_recv.at[pl.ds(0, DEVICES - 1)], ret_send_sem)

    @pl.when(jnp.logical_not(is_owner))
    def _():
        wait_bytes(send, send_sem)
        wait_bytes(lab_send, lab_send_sem)


def on_device(emb, cluster, owner_of):
    best = pl.pallas_call(
        kernel,
        out_shape=jax.ShapeDtypeStruct((1, ROWS), jnp.float32),
        in_specs=[pl.BlockSpec(memory_space=pltpu.HBM)] * 3,
        out_specs=pl.BlockSpec(memory_space=pltpu.VMEM),
        scratch_shapes=[
            pltpu.VMEM((ROWS, WIDTH), jnp.bfloat16),
            pltpu.VMEM((1, ROWS), jnp.int32),
            pltpu.VMEM((1, CLUSTERS), jnp.int32),
            pltpu.VMEM((OWNERS, 2 * CAP, HALF), jnp.bfloat16),
            pltpu.VMEM((OWNERS, 128), jnp.float32),
            pltpu.VMEM((DEVICES, 2 * CAP, HALF), jnp.bfloat16),
            pltpu.VMEM((DEVICES, 128), jnp.float32),
            pltpu.VMEM((DEVICES * CAP, WIDTH), jnp.bfloat16),
            pltpu.VMEM((2, 128), jnp.float32),
            pltpu.VMEM((8, 128), jnp.float32),
            pltpu.VMEM((OWNERS, 128), jnp.float32),
            pltpu.SemaphoreType.DMA((3,)),
            pltpu.SemaphoreType.DMA,
            pltpu.SemaphoreType.DMA,
            pltpu.SemaphoreType.DMA,
            pltpu.SemaphoreType.DMA((2,)),
            pltpu.SemaphoreType.DMA,
            pltpu.SemaphoreType.DMA,
        ],
        compiler_params=pltpu.CompilerParams(
            collective_id=0, has_side_effects=True, vmem_limit_bytes=24 * 1024 * 1024
        ),
    )(*[
        pltpu.with_memory_space_constraint(a, pltpu.HBM)
        for a in (emb, cluster.reshape(1, ROWS), owner_of.reshape(1, CLUSTERS))
    ])
    return best.reshape(ROWS)


def solution(mesh):
    return jax.shard_map(
        on_device,
        mesh=mesh,
        in_specs=(P(("owner", "split"), None), P(("owner", "split")), P()),
        out_specs=P(("owner", "split")),
        check_vma=False,
    )
```

```python
import jax
import jax.numpy as jnp
from jax import lax
from jax.experimental import pallas as pl
from jax.experimental.pallas import tpu as pltpu
from jax.sharding import PartitionSpec as P

MESH = pl.DeviceIdType.MESH
OWNERS = 32
SPLITS = 4
CAP = 8
WIDTH = 1024
HALF = WIDTH // 2
ROWS = 128
CLUSTERS = 64
NEARS = ((0, 0), (1, 0), (0, 1), (3, 0), (0, 3), (1, 1), (2, 0), (0, 2))
NEARS3 = ()
FAR_CORE = 0
FAR_DX = (2, 1, 3, 0)
FAR_DY = (2, 1, 3, 0)
DEVICES = OWNERS * SPLITS
GROUPS = 4
PER = DEVICES // GROUPS
GROUP_ROWS = PER * CAP
UNROLL = 4
MULT = 1
SPIN_X = 4
SPIN_M = 8


def home_of(o):
    return lax.div(o, 4) * 2 + 1, lax.rem(o, 4)


def iota(shape, dim):
    return lax.broadcasted_iota(jnp.int32, shape, dim)


def wait_bytes(ref, sem):
    pltpu.make_async_copy(ref, ref, sem).wait()


def is_near(x, y, z, core):
    near = z < 0
    for plane, columns in ((2, NEARS), (3, NEARS3)):
        for a, b in columns:
            near = near | ((x == a) & (y == b) & ((z == plane) | (z == 3 - plane)))
    return near & (core == FAR_CORE)


def spot_of(z, y, core, x):
    return (
        lax.div(z, 2) * 64 + lax.div(y, 2) * 32 + lax.div(x, 2) * 16
        + lax.rem(y, 2) * 8 + lax.rem(x, 2) * 4 + lax.rem(z, 2) * 2 + core
    )


def find_slots(cluster, owners, lane):
    hot = (iota((CLUSTERS, ROWS), 0) == cluster).astype(jnp.bfloat16)
    table = (iota((OWNERS, CLUSTERS), 0) == owners).astype(jnp.bfloat16)
    owner_hot = jnp.dot(table, hot, preferred_element_type=jnp.float32)
    before = (iota((ROWS, ROWS), 0) < iota((ROWS, ROWS), 1)).astype(jnp.bfloat16)
    count = jnp.dot(owner_hot.astype(jnp.bfloat16), before, preferred_element_type=jnp.float32)
    slot = jnp.sum(
        owner_hot * (count + CAP * iota((OWNERS, ROWS), 0).astype(jnp.float32)), 0, keepdims=True
    ).astype(jnp.int32)
    lane_hot = iota((ROWS, ROWS), 0) == lane + (slot & (CAP - 1))
    return owner_hot, slot, lane_hot


def fill(values, cluster, owner_hot, slot, lane_hot, send, lab_send):
    labels = (owner_hot * (cluster + 1).astype(jnp.float32)).astype(jnp.bfloat16)
    lab_send[...] = lax.dot_general(
        labels, lane_hot.astype(jnp.bfloat16), (((1,), (1,)), ((), ())),
        preferred_element_type=jnp.float32,
    )
    values = values.astype(jnp.float32)
    unit = (values * lax.rsqrt(jnp.sum(values * values, 1, keepdims=True) + 1e-06)).astype(jnp.bfloat16)
    pick = (iota((OWNERS * CAP, ROWS), 0) == slot).astype(jnp.bfloat16)
    parts = [
        jnp.dot(pick, unit[:, h * HALF:(h + 1) * HALF], preferred_element_type=jnp.float32).reshape(
            OWNERS, CAP, HALF
        )
        for h in range(2)
    ]
    send[...] = jnp.concatenate(parts, 1).astype(jnp.bfloat16)


def kernel(
    emb_hbm, clu_hbm, own_hbm, out_ref,
    emb_ref, clu_ref, own_ref, send, lab_send, emb_far, clu_far, send_far, lab_far, recv, lab_recv, held, soon, best, ret_recv,
    load_sem, send_sem, lab_send_sem, ret_send_sem, recv_sem, lab_sem, ret_sem,
    far_send_sem, lab_far_sem, give_sem, got_sem,
):
    me = lax.axis_index("owner")
    split = lax.axis_index("split")
    z, y, core = lax.div(me, 8), lax.rem(lax.div(me, 2), 4), lax.rem(me, 2)
    here = spot_of(z, y, core, split)
    near = is_near(split, y, z, core)
    is_relay = (z < 2) & near
    is_far = (z >= 2) & near
    peer = ((3 - z) * 8 + y * 2 + core, split)
    is_owner = (lax.rem(me, 2) == 1) & (me < 16)
    mine = lax.rem(lax.div(me, 2), 8) * 4 + split
    loads = [
        pltpu.make_async_copy(src, dst, load_sem.at[i])
        for i, (src, dst) in enumerate(((clu_hbm, clu_ref), (own_hbm, own_ref), (emb_hbm, emb_ref)))
    ]
    for load in loads:
        load.start()
    barrier = pltpu.get_barrier_semaphore()

    @pl.when(is_relay)
    def _():
        pl.semaphore_signal(barrier, inc=1, device_id=peer, device_id_type=MESH)

    @pl.when(is_owner)
    def _():
        def greet(t, c):
            to = OWNERS - 1 - t
            for q in range(SPLITS):
                ahead = (to >= 16) & is_near(q, lax.rem(lax.div(to, 2), 4), lax.div(to, 8), lax.rem(to, 2))

                @pl.when(jnp.logical_not(ahead | ((to == me) & (q == split))))
                def _():
                    pl.semaphore_signal(barrier, inc=1, device_id=(to, q), device_id_type=MESH)
            return c
        lax.fori_loop(0, OWNERS, greet, 0, unroll=UNROLL)

    far_copies = [
        pltpu.make_async_remote_copy(
            src_ref=src, dst_ref=dst, send_sem=give_sem.at[i], recv_sem=got_sem.at[i],
            device_id=peer, device_id_type=MESH,
        )
        for i, (src, dst) in enumerate(((clu_hbm, clu_far), (emb_hbm, emb_far)))
    ]

    @pl.when(is_far)
    def _():
        pl.semaphore_wait(barrier, 1)
        for copy in far_copies:
            copy.start()

    loads[0].wait()
    loads[1].wait()
    cluster = clu_ref[...]
    owner_hot, slot, lane_hot = find_slots(cluster, own_ref[...], lax.rem(here, 16) * CAP)
    loads[2].wait()

    @pl.when(jnp.logical_not(is_far))
    def _():
        fill(emb_ref[...], cluster, owner_hot, slot, lane_hot, send, lab_send)

    @pl.when(jnp.logical_not(is_far))
    def _():
        pl.semaphore_wait(barrier, jnp.where(is_owner, OWNERS - 1, OWNERS))

    first = lax.rem(SPIN_X * split + SPIN_M * me, OWNERS)

    def send_step(o, spot, rows, labels, rows_sem, labels_sem):
        there = home_of(o)
        pltpu.make_async_remote_copy(
            src_ref=labels.at[pl.ds(o, 1)], dst_ref=lab_recv.at[pl.ds(spot, 1)],
            send_sem=labels_sem, recv_sem=lab_sem, device_id=there, device_id_type=MESH,
        ).start()
        pltpu.make_async_remote_copy(
            src_ref=rows.at[o], dst_ref=recv.at[spot],
            send_sem=rows_sem, recv_sem=recv_sem.at[lax.div(spot, 64)], device_id=there, device_id_type=MESH,
        ).start()

    @pl.when(jnp.logical_not(is_far))
    def _():
        def post(t, c):
            o = lax.rem(first + MULT * t, OWNERS)

            @pl.when(jnp.logical_not(is_owner & (o == mine)))
            def _():
                send_step(o, here, send, lab_send, send_sem, lab_send_sem)
            return c
        lax.fori_loop(0, OWNERS, post, 0, unroll=UNROLL)

    @pl.when(is_relay)
    def _():
        for copy in far_copies:
            copy.wait_recv()
        cluster = clu_far[...]
        spot = spot_of(3 - z, y, core, split)
        fill(
            emb_far[...], cluster, *find_slots(cluster, own_ref[...], lax.rem(spot, 16) * CAP), send_far, lab_far
        )
        for dx in FAR_DX:
            for dy in FAR_DY:
                for plane in range(2):
                    o = plane * 16 + lax.rem(y + dy, 4) * 4 + lax.rem(split + dx, 4)
                    send_step(o, spot, send_far, lab_far, far_send_sem, lab_far_sem)

    @pl.when(is_owner)
    def _():
        recv[here] = send[mine]
        lab_recv[pl.ds(here, 1)] = lab_send[pl.ds(mine, 1)]
        wait_bytes(lab_recv.at[pl.ds(0, DEVICES - 1)], lab_sem)
        labels = jnp.sum(lab_recv[...].reshape(8, 16, 128), 1)
        eye = iota((ROWS, ROWS), 0) == iota((ROWS, ROWS), 1)
        columns = lax.dot_general(
            eye.astype(jnp.bfloat16), labels.astype(jnp.bfloat16), (((1,), (1,)), ((), ())),
            preferred_element_type=jnp.float32,
        )
        tops, wides = [None] * 8, [None] * 8

        def take(begin, end):
            got = recv[begin // CAP:end // CAP].astype(jnp.float32)
            for h in range(2):
                held[begin:end, h * HALF:(h + 1) * HALF] = (
                    got[:, h * CAP:(h + 1) * CAP].reshape(end - begin, HALF).astype(jnp.bfloat16)
                )

        def score(rows, cols):
            scores = lax.dot_general(
                held[rows[0] * 128:rows[1] * 128, :], held[cols[0] * 128:cols[1] * 128, :],
                (((1,), (1,)), ((), ())), preferred_element_type=jnp.float32,
            )
            for i in range(*rows):
                for j in range(*cols):
                    same = columns[:, i:i + 1] == labels[j:j + 1, :]
                    if i == j:
                        same = same & jnp.logical_not(eye)
                    u, v = (i - rows[0]) * 128, (j - cols[0]) * 128
                    kept = jnp.where(same, scores[u:u + 128, v:v + 128], -2.0)
                    top = jnp.max(kept, 0, keepdims=True)
                    tops[j] = top if tops[j] is None else jnp.maximum(tops[j], top)
                    if not cols[0] <= i < cols[1]:
                        wides[i] = kept if wides[i] is None else jnp.maximum(wides[i], kept)

        def close(i):
            if wides[i] is not None:
                tops[i] = jnp.maximum(tops[i], jnp.max(jnp.transpose(wides[i]), 0, keepdims=True))

        def give(src, m, x):
            @pl.when(jnp.logical_not((m == me) & (x == split)))
            def _():
                pltpu.make_async_remote_copy(
                    src_ref=src, dst_ref=ret_recv.at[pl.ds(mine, 1)],
                    send_sem=ret_send_sem, recv_sem=ret_sem, device_id=(m, x), device_id_type=MESH,
                ).start()

        wait_bytes(recv.at[pl.ds(0, DEVICES // 2 - 1)], recv_sem.at[0])
        take(0, 512)
        score((0, 2), (0, 2))
        score((0, 4), (2, 4))
        close(0)
        close(1)
        wait_bytes(recv.at[pl.ds(0, DEVICES // 2)], recv_sem.at[1])
        take(512, 1024)
        score((4, 8), (0, 2))
        for b in range(2):
            soon[b:b + 1, :] = tops[b]
        for m in (1, 0, 9, 8, 3, 2, 11, 10):
            for x in range(SPLITS):
                give(soon.at[pl.ds(x // 2, 1)], m, x)
        score((4, 8), (2, 4))
        score((4, 6), (4, 6))
        score((4, 8), (6, 8))
        for b in range(4, 6):
            close(b)
        for b in range(6, 8):
            close(b)
        for b in range(8):
            best[b:b + 1, :] = tops[b]

        def give_row(m, c):
            z_to, y_to = lax.div(m, 8), lax.rem(lax.div(m, 2), 4)
            block = lax.div(z_to, 2) * 4 + lax.div(y_to, 2) * 2

            @pl.when(block != 0)
            def _():
                for x in range(SPLITS):
                    give(best.at[pl.ds(block + x // 2, 1)], m, x)
            return c
        lax.fori_loop(0, OWNERS, give_row, 0)
        ret_recv[pl.ds(mine, 1)] = best[pl.ds(lax.div(here, 16), 1)]
        wait_bytes(ret_recv.at[pl.ds(0, OWNERS - 1)], ret_sem)

    @pl.when(jnp.logical_not(is_owner))
    def _():
        wait_bytes(ret_recv, ret_sem)
    rest = ret_recv[...]
    terms = []
    for _ in range(3):
        terms.append(rest.astype(jnp.bfloat16))
        rest = rest - terms[-1].astype(jnp.float32)
    spread = lax.dot_general(
        jnp.concatenate(terms, 0), jnp.concatenate([owner_hot.astype(jnp.bfloat16)] * 3, 0),
        (((0,), (0,)), ((), ())), preferred_element_type=jnp.float32,
    )
    out_ref[...] = jnp.sum(jnp.where(lane_hot, spread, 0.0), 0, keepdims=True)
    @pl.when(is_owner)
    def _():
        wait_bytes(send.at[pl.ds(0, OWNERS - 1)], send_sem)
        wait_bytes(lab_send.at[pl.ds(0, OWNERS - 1)], lab_send_sem)
        wait_bytes(lab_recv.at[pl.ds(0, DEVICES - 1)], ret_send_sem)

    @pl.when(jnp.logical_not(is_owner | is_far))
    def _():
        wait_bytes(send, send_sem)
        wait_bytes(lab_send, lab_send_sem)

    @pl.when(is_far)
    def _():
        for copy in far_copies:
            copy.wait_send()

    @pl.when(is_relay)
    def _():
        wait_bytes(send_far, far_send_sem)
        wait_bytes(lab_far, lab_far_sem)


def on_device(emb, cluster, owner_of):
    best = pl.pallas_call(
        kernel,
        out_shape=jax.ShapeDtypeStruct((1, ROWS), jnp.float32),
        in_specs=[pl.BlockSpec(memory_space=pltpu.HBM)] * 3,
        out_specs=pl.BlockSpec(memory_space=pltpu.VMEM),
        scratch_shapes=[
            pltpu.VMEM((ROWS, WIDTH), jnp.bfloat16),
            pltpu.VMEM((1, ROWS), jnp.int32),
            pltpu.VMEM((1, CLUSTERS), jnp.int32),
            pltpu.VMEM((OWNERS, 2 * CAP, HALF), jnp.bfloat16),
            pltpu.VMEM((OWNERS, 128), jnp.float32),
            pltpu.VMEM((ROWS, WIDTH), jnp.bfloat16),
            pltpu.VMEM((1, ROWS), jnp.int32),
            pltpu.VMEM((OWNERS, 2 * CAP, HALF), jnp.bfloat16),
            pltpu.VMEM((OWNERS, 128), jnp.float32),
            pltpu.VMEM((DEVICES, 2 * CAP, HALF), jnp.bfloat16),
            pltpu.VMEM((DEVICES, 128), jnp.float32),
            pltpu.VMEM((DEVICES * CAP, WIDTH), jnp.bfloat16),
            pltpu.VMEM((2, 128), jnp.float32),
            pltpu.VMEM((8, 128), jnp.float32),
            pltpu.VMEM((OWNERS, 128), jnp.float32),
            pltpu.SemaphoreType.DMA((3,)),
            pltpu.SemaphoreType.DMA,
            pltpu.SemaphoreType.DMA,
            pltpu.SemaphoreType.DMA,
            pltpu.SemaphoreType.DMA((2,)),
            pltpu.SemaphoreType.DMA,
            pltpu.SemaphoreType.DMA,
            pltpu.SemaphoreType.DMA,
            pltpu.SemaphoreType.DMA,
            pltpu.SemaphoreType.DMA((2,)),
            pltpu.SemaphoreType.DMA((2,)),
        ],
        compiler_params=pltpu.CompilerParams(
            collective_id=0, has_side_effects=True, vmem_limit_bytes=24 * 1024 * 1024
        ),
    )(*[
        pltpu.with_memory_space_constraint(a, pltpu.HBM)
        for a in (emb, cluster.reshape(1, ROWS), owner_of.reshape(1, CLUSTERS))
    ])
    return best.reshape(ROWS)


def solution(mesh):
    return jax.shard_map(
        on_device,
        mesh=mesh,
        in_specs=(P(("owner", "split"), None), P(("owner", "split")), P()),
        out_specs=P(("owner", "split")),
        check_vma=False,
    )
```

```python
import jax
import jax.numpy as jnp
from jax import lax
from jax.experimental import pallas as pl
from jax.experimental.pallas import tpu as pltpu
from jax.sharding import PartitionSpec as P

MESH = pl.DeviceIdType.MESH
OWNERS = 32
SPLITS = 4
CAP = 8
WIDTH = 1024
HALF = WIDTH // 2
ROWS = 128
CLUSTERS = 64
FAR_DX = (2, 1, 3, 0)
FAR_DY = (2, 1, 3, 0)
DEVICES = OWNERS * SPLITS
GROUPS = 4
PER = DEVICES // GROUPS
GROUP_ROWS = PER * CAP
UNROLL = 4
PN = 12
SPIN_X = 4
SPIN_M = 8


def home_of(o):
    return lax.div(o, 4) * 2 + 1, lax.rem(o, 4)


def iota(shape, dim):
    return lax.broadcasted_iota(jnp.int32, shape, dim)


def wait_bytes(ref, sem):
    pltpu.make_async_copy(ref, ref, sem).wait()


def spot_of(z, y, core, x):
    return (
        lax.div(z, 2) * 64 + lax.div(y, 2) * 32 + lax.div(x, 2) * 16
        + lax.rem(y, 2) * 8 + lax.rem(x, 2) * 4 + lax.rem(z, 2) * 2 + core
    )


def find_slots(cluster, owners, lane):
    hot = (iota((CLUSTERS, ROWS), 0) == cluster).astype(jnp.bfloat16)
    table = (iota((OWNERS, CLUSTERS), 0) == owners).astype(jnp.bfloat16)
    owner_hot = jnp.dot(table, hot, preferred_element_type=jnp.float32)
    before = (iota((ROWS, ROWS), 0) < iota((ROWS, ROWS), 1)).astype(jnp.bfloat16)
    count = jnp.dot(owner_hot.astype(jnp.bfloat16), before, preferred_element_type=jnp.float32)
    slot = jnp.sum(
        owner_hot * (count + CAP * iota((OWNERS, ROWS), 0).astype(jnp.float32)), 0, keepdims=True
    ).astype(jnp.int32)
    lane_hot = iota((ROWS, ROWS), 0) == lane + (slot & (CAP - 1))
    return owner_hot, slot, lane_hot


def fill(values, cluster, owner_hot, slot, lane_hot, send, lab_send):
    labels = (owner_hot * (cluster + 1).astype(jnp.float32)).astype(jnp.bfloat16)
    lab_send[...] = lax.dot_general(
        labels, lane_hot.astype(jnp.bfloat16), (((1,), (1,)), ((), ())),
        preferred_element_type=jnp.float32,
    )
    values = values.astype(jnp.float32)
    unit = (values * lax.rsqrt(jnp.sum(values * values, 1, keepdims=True) + 1e-06)).astype(jnp.bfloat16)
    pick = (iota((OWNERS * CAP, ROWS), 0) == slot).astype(jnp.bfloat16)
    parts = [
        jnp.dot(pick, unit[:, h * HALF:(h + 1) * HALF], preferred_element_type=jnp.float32).reshape(
            OWNERS, CAP, HALF
        )
        for h in range(2)
    ]
    send[...] = jnp.concatenate(parts, 1).astype(jnp.bfloat16)


def kernel(
    emb_hbm, clu_hbm, own_hbm, out_ref,
    emb_ref, clu_ref, own_ref, send, lab_send, emb_far, clu_far, send_far, lab_far, recv, lab_recv, held, soon, best, ret_recv,
    load_sem, send_sem, lab_send_sem, ret_send_sem, recv_sem, lab_sem, ret_sem,
    far_send_sem, lab_far_sem, give_sem, got_sem,
):
    me = lax.axis_index("owner")
    split = lax.axis_index("split")
    z, y, core = lax.div(me, 8), lax.rem(lax.div(me, 2), 4), lax.rem(me, 2)
    here = spot_of(z, y, core, split)
    is_far = (z == 2) & (core == 0)
    is_relay = (z == 1) & (core == 0)
    is_paced = (z >= 2) & (core == 1)
    peer = ((3 - z) * 8 + y * 2 + core, split)
    is_owner = (lax.rem(me, 2) == 1) & (me < 16)
    mine = lax.rem(lax.div(me, 2), 8) * 4 + split
    loads = [
        pltpu.make_async_copy(src, dst, load_sem.at[i])
        for i, (src, dst) in enumerate(((clu_hbm, clu_ref), (own_hbm, own_ref), (emb_hbm, emb_ref)))
    ]
    for load in loads:
        load.start()
    barrier = pltpu.get_barrier_semaphore()

    @pl.when(is_relay)
    def _():
        pl.semaphore_signal(barrier, inc=1, device_id=peer, device_id_type=MESH)

    @pl.when(is_owner)
    def _():
        def greet(t, c):
            to = OWNERS - 1 - t
            for q in range(SPLITS):
                ahead = (lax.div(to, 8) == 2) & (lax.rem(to, 2) == 0)

                @pl.when(jnp.logical_not(ahead | ((to == me) & (q == split))))
                def _():
                    pl.semaphore_signal(barrier, inc=1, device_id=(to, q), device_id_type=MESH)
            return c
        lax.fori_loop(0, OWNERS, greet, 0, unroll=UNROLL)

    far_copies = [
        pltpu.make_async_remote_copy(
            src_ref=src, dst_ref=dst, send_sem=give_sem.at[i], recv_sem=got_sem.at[i],
            device_id=peer, device_id_type=MESH,
        )
        for i, (src, dst) in enumerate(((clu_hbm, clu_far), (emb_hbm, emb_far)))
    ]

    @pl.when(is_far)
    def _():
        pl.semaphore_wait(barrier, 1)
        for copy in far_copies:
            copy.start()

    loads[0].wait()
    loads[1].wait()
    cluster = clu_ref[...]
    owner_hot, slot, lane_hot = find_slots(cluster, own_ref[...], lax.rem(here, 16) * CAP)
    loads[2].wait()

    @pl.when(jnp.logical_not(is_far))
    def _():
        fill(emb_ref[...], cluster, owner_hot, slot, lane_hot, send, lab_send)

    @pl.when(jnp.logical_not(is_far))
    def _():
        pl.semaphore_wait(barrier, jnp.where(is_owner, OWNERS - 1, OWNERS))

    first = lax.rem(SPIN_X * split + SPIN_M * me, OWNERS)

    def send_step(o, spot, rows, labels, rows_sem, labels_sem):
        there = home_of(o)
        pltpu.make_async_remote_copy(
            src_ref=labels.at[pl.ds(o, 1)], dst_ref=lab_recv.at[pl.ds(spot, 1)],
            send_sem=labels_sem, recv_sem=lab_sem, device_id=there, device_id_type=MESH,
        ).start()
        pltpu.make_async_remote_copy(
            src_ref=rows.at[o], dst_ref=recv.at[spot],
            send_sem=rows_sem, recv_sem=recv_sem.at[lax.div(spot, 64)], device_id=there, device_id_type=MESH,
        ).start()

    @pl.when(jnp.logical_not(is_far))
    def _():
        def post(t, c):
            o = jnp.where(z >= 2, lax.div(t, 16) * 16 + lax.rem(first + t, 16), lax.rem(first + t, OWNERS))

            @pl.when(jnp.logical_not(is_owner & (o == mine)))
            def _():
                send_step(o, here, send, lab_send, send_sem, lab_send_sem)
            return c
        lax.fori_loop(0, PN, post, 0, unroll=UNROLL)

        @pl.when(is_paced)
        def _():
            wait_bytes(send.at[pl.ds(0, PN)], send_sem)
        lax.fori_loop(PN, OWNERS, post, 0, unroll=UNROLL)

    @pl.when(is_relay)
    def _():
        for copy in far_copies:
            copy.wait_recv()
        cluster = clu_far[...]
        spot = spot_of(3 - z, y, core, split)
        fill(
            emb_far[...], cluster, *find_slots(cluster, own_ref[...], lax.rem(spot, 16) * CAP), send_far, lab_far
        )
        for dx in FAR_DX:
            for dy in FAR_DY:
                for plane in range(2):
                    o = plane * 16 + lax.rem(y + dy, 4) * 4 + lax.rem(split + dx, 4)
                    send_step(o, spot, send_far, lab_far, far_send_sem, lab_far_sem)

    @pl.when(is_owner)
    def _():
        recv[here] = send[mine]
        lab_recv[pl.ds(here, 1)] = lab_send[pl.ds(mine, 1)]
        wait_bytes(lab_recv.at[pl.ds(0, DEVICES - 1)], lab_sem)
        labels = jnp.sum(lab_recv[...].reshape(8, 16, 128), 1)
        eye = iota((ROWS, ROWS), 0) == iota((ROWS, ROWS), 1)
        columns = lax.dot_general(
            eye.astype(jnp.bfloat16), labels.astype(jnp.bfloat16), (((1,), (1,)), ((), ())),
            preferred_element_type=jnp.float32,
        )
        tops, wides = [None] * 8, [None] * 8

        def take(begin, end):
            got = recv[begin // CAP:end // CAP].astype(jnp.float32)
            for h in range(2):
                held[begin:end, h * HALF:(h + 1) * HALF] = (
                    got[:, h * CAP:(h + 1) * CAP].reshape(end - begin, HALF).astype(jnp.bfloat16)
                )

        def score(rows, cols):
            scores = lax.dot_general(
                held[rows[0] * 128:rows[1] * 128, :], held[cols[0] * 128:cols[1] * 128, :],
                (((1,), (1,)), ((), ())), preferred_element_type=jnp.float32,
            )
            for i in range(*rows):
                for j in range(*cols):
                    same = columns[:, i:i + 1] == labels[j:j + 1, :]
                    if i == j:
                        same = same & jnp.logical_not(eye)
                    u, v = (i - rows[0]) * 128, (j - cols[0]) * 128
                    kept = jnp.where(same, scores[u:u + 128, v:v + 128], -2.0)
                    top = jnp.max(kept, 0, keepdims=True)
                    tops[j] = top if tops[j] is None else jnp.maximum(tops[j], top)
                    if not cols[0] <= i < cols[1]:
                        wides[i] = kept if wides[i] is None else jnp.maximum(wides[i], kept)

        def close(i):
            if wides[i] is not None:
                tops[i] = jnp.maximum(tops[i], jnp.max(jnp.transpose(wides[i]), 0, keepdims=True))

        def give(src, m, x):
            @pl.when(jnp.logical_not((m == me) & (x == split)))
            def _():
                pltpu.make_async_remote_copy(
                    src_ref=src, dst_ref=ret_recv.at[pl.ds(mine, 1)],
                    send_sem=ret_send_sem, recv_sem=ret_sem, device_id=(m, x), device_id_type=MESH,
                ).start()

        wait_bytes(recv.at[pl.ds(0, DEVICES // 2 - 1)], recv_sem.at[0])
        take(0, 512)
        score((0, 2), (0, 2))
        score((0, 4), (2, 4))
        close(0)
        close(1)
        wait_bytes(recv.at[pl.ds(0, DEVICES // 2)], recv_sem.at[1])
        take(512, 1024)
        score((4, 8), (0, 2))
        for b in range(2):
            soon[b:b + 1, :] = tops[b]
        for m in (1, 0, 9, 8, 3, 2, 11, 10):
            for x in range(SPLITS):
                give(soon.at[pl.ds(x // 2, 1)], m, x)
        score((4, 8), (2, 4))
        score((4, 6), (4, 6))
        score((4, 8), (6, 8))
        for b in range(4, 6):
            close(b)
        for b in range(6, 8):
            close(b)
        for b in range(8):
            best[b:b + 1, :] = tops[b]

        def give_row(m, c):
            z_to, y_to = lax.div(m, 8), lax.rem(lax.div(m, 2), 4)
            block = lax.div(z_to, 2) * 4 + lax.div(y_to, 2) * 2

            @pl.when(block != 0)
            def _():
                for x in range(SPLITS):
                    give(best.at[pl.ds(block + x // 2, 1)], m, x)
            return c
        lax.fori_loop(0, OWNERS, give_row, 0)
        ret_recv[pl.ds(mine, 1)] = best[pl.ds(lax.div(here, 16), 1)]
        wait_bytes(ret_recv.at[pl.ds(0, OWNERS - 1)], ret_sem)

    @pl.when(jnp.logical_not(is_owner))
    def _():
        wait_bytes(ret_recv, ret_sem)
    rest = ret_recv[...]
    terms = []
    for _ in range(3):
        terms.append(rest.astype(jnp.bfloat16))
        rest = rest - terms[-1].astype(jnp.float32)
    spread = lax.dot_general(
        jnp.concatenate(terms, 0), jnp.concatenate([owner_hot.astype(jnp.bfloat16)] * 3, 0),
        (((0,), (0,)), ((), ())), preferred_element_type=jnp.float32,
    )
    out_ref[...] = jnp.sum(jnp.where(lane_hot, spread, 0.0), 0, keepdims=True)
    @pl.when(is_owner)
    def _():
        wait_bytes(send.at[pl.ds(0, OWNERS - 1)], send_sem)
        wait_bytes(lab_send.at[pl.ds(0, OWNERS - 1)], lab_send_sem)
        wait_bytes(lab_recv.at[pl.ds(0, DEVICES - 1)], ret_send_sem)

    @pl.when(jnp.logical_not(is_owner | is_far))
    def _():
        @pl.when(is_paced)
        def _():
            wait_bytes(send.at[pl.ds(0, OWNERS - PN)], send_sem)

        @pl.when(jnp.logical_not(is_paced))
        def _():
            wait_bytes(send, send_sem)
        wait_bytes(lab_send, lab_send_sem)

    @pl.when(is_far)
    def _():
        for copy in far_copies:
            copy.wait_send()

    @pl.when(is_relay)
    def _():
        wait_bytes(send_far, far_send_sem)
        wait_bytes(lab_far, lab_far_sem)


def on_device(emb, cluster, owner_of):
    best = pl.pallas_call(
        kernel,
        out_shape=jax.ShapeDtypeStruct((1, ROWS), jnp.float32),
        in_specs=[pl.BlockSpec(memory_space=pltpu.HBM)] * 3,
        out_specs=pl.BlockSpec(memory_space=pltpu.VMEM),
        scratch_shapes=[
            pltpu.VMEM((ROWS, WIDTH), jnp.bfloat16),
            pltpu.VMEM((1, ROWS), jnp.int32),
            pltpu.VMEM((1, CLUSTERS), jnp.int32),
            pltpu.VMEM((OWNERS, 2 * CAP, HALF), jnp.bfloat16),
            pltpu.VMEM((OWNERS, 128), jnp.float32),
            pltpu.VMEM((ROWS, WIDTH), jnp.bfloat16),
            pltpu.VMEM((1, ROWS), jnp.int32),
            pltpu.VMEM((OWNERS, 2 * CAP, HALF), jnp.bfloat16),
            pltpu.VMEM((OWNERS, 128), jnp.float32),
            pltpu.VMEM((DEVICES, 2 * CAP, HALF), jnp.bfloat16),
            pltpu.VMEM((DEVICES, 128), jnp.float32),
            pltpu.VMEM((DEVICES * CAP, WIDTH), jnp.bfloat16),
            pltpu.VMEM((2, 128), jnp.float32),
            pltpu.VMEM((8, 128), jnp.float32),
            pltpu.VMEM((OWNERS, 128), jnp.float32),
            pltpu.SemaphoreType.DMA((3,)),
            pltpu.SemaphoreType.DMA,
            pltpu.SemaphoreType.DMA,
            pltpu.SemaphoreType.DMA,
            pltpu.SemaphoreType.DMA((2,)),
            pltpu.SemaphoreType.DMA,
            pltpu.SemaphoreType.DMA,
            pltpu.SemaphoreType.DMA,
            pltpu.SemaphoreType.DMA,
            pltpu.SemaphoreType.DMA((2,)),
            pltpu.SemaphoreType.DMA((2,)),
        ],
        compiler_params=pltpu.CompilerParams(
            collective_id=0, has_side_effects=True, vmem_limit_bytes=24 * 1024 * 1024
        ),
    )(*[
        pltpu.with_memory_space_constraint(a, pltpu.HBM)
        for a in (emb, cluster.reshape(1, ROWS), owner_of.reshape(1, CLUSTERS))
    ])
    return best.reshape(ROWS)


def solution(mesh):
    return jax.shard_map(
        on_device,
        mesh=mesh,
        in_specs=(P(("owner", "split"), None), P(("owner", "split")), P()),
        out_specs=P(("owner", "split")),
        check_vma=False,
    )
```

```python
import jax
import jax.numpy as jnp
from jax import lax
from jax.experimental import pallas as pl
from jax.experimental.pallas import tpu as pltpu
from jax.sharding import PartitionSpec as P

MESH = pl.DeviceIdType.MESH
OWNERS = 32
SPLITS = 4
CAP = 8
WIDTH = 1024
HALF = WIDTH // 2
ROWS = 128
CLUSTERS = 64
FAR_DX = (2, 1, 3, 0)
FAR_DY = (2, 1, 3, 0)
DEVICES = OWNERS * SPLITS
GROUPS = 4
PER = DEVICES // GROUPS
GROUP_ROWS = PER * CAP
UNROLL = 4
PN = 16
SPIN_X = 4
SPIN_M = 8


def home_of(o):
    return lax.div(o, 4) * 2 + 1, lax.rem(o, 4)


def iota(shape, dim):
    return lax.broadcasted_iota(jnp.int32, shape, dim)


def wait_bytes(ref, sem):
    pltpu.make_async_copy(ref, ref, sem).wait()


def spot_of(z, y, core, x):
    return (
        lax.div(z, 2) * 64 + lax.div(y, 2) * 32 + lax.div(x, 2) * 16
        + lax.rem(y, 2) * 8 + lax.rem(x, 2) * 4 + lax.rem(z, 2) * 2 + core
    )


def find_slots(cluster, owners, lane):
    hot = (iota((CLUSTERS, ROWS), 0) == cluster).astype(jnp.bfloat16)
    table = (iota((OWNERS, CLUSTERS), 0) == owners).astype(jnp.bfloat16)
    owner_hot = jnp.dot(table, hot, preferred_element_type=jnp.float32)
    before = (iota((ROWS, ROWS), 0) < iota((ROWS, ROWS), 1)).astype(jnp.bfloat16)
    count = jnp.dot(owner_hot.astype(jnp.bfloat16), before, preferred_element_type=jnp.float32)
    slot = jnp.sum(
        owner_hot * (count + CAP * iota((OWNERS, ROWS), 0).astype(jnp.float32)), 0, keepdims=True
    ).astype(jnp.int32)
    lane_hot = iota((ROWS, ROWS), 0) == lane + (slot & (CAP - 1))
    return owner_hot, slot, lane_hot


def fill(values, cluster, owner_hot, slot, lane_hot, send, lab_send):
    labels = (owner_hot * (cluster + 1).astype(jnp.float32)).astype(jnp.bfloat16)
    lab_send[...] = lax.dot_general(
        labels, lane_hot.astype(jnp.bfloat16), (((1,), (1,)), ((), ())),
        preferred_element_type=jnp.float32,
    )
    values = values.astype(jnp.float32)
    unit = (values * lax.rsqrt(jnp.sum(values * values, 1, keepdims=True) + 1e-06)).astype(jnp.bfloat16)
    pick = (iota((OWNERS * CAP, ROWS), 0) == slot).astype(jnp.bfloat16)
    parts = [
        jnp.dot(pick, unit[:, h * HALF:(h + 1) * HALF], preferred_element_type=jnp.float32).reshape(
            OWNERS, CAP, HALF
        )
        for h in range(2)
    ]
    send[...] = jnp.concatenate(parts, 1).astype(jnp.bfloat16)


def kernel(
    emb_hbm, clu_hbm, own_hbm, out_ref,
    emb_ref, clu_ref, own_ref, send, lab_send, emb_far, clu_far, send_far, lab_far, recv, lab_recv, held, soon, best, ret_recv,
    load_sem, send_sem, lab_send_sem, ret_send_sem, recv_sem, lab_sem, ret_sem,
    far_send_sem, lab_far_sem, give_sem, got_sem,
):
    me = lax.axis_index("owner")
    split = lax.axis_index("split")
    z, y, core = lax.div(me, 8), lax.rem(lax.div(me, 2), 4), lax.rem(me, 2)
    here = spot_of(z, y, core, split)
    is_far = (z == 2) & (core == 0)
    is_relay = (z == 1) & (core == 0)
    is_paced = (z >= 2) & (core == 1)
    peer = ((3 - z) * 8 + y * 2 + core, split)
    is_owner = (lax.rem(me, 2) == 1) & (me < 16)
    mine = lax.rem(lax.div(me, 2), 8) * 4 + split
    loads = [
        pltpu.make_async_copy(src, dst, load_sem.at[i])
        for i, (src, dst) in enumerate(((clu_hbm, clu_ref), (own_hbm, own_ref), (emb_hbm, emb_ref)))
    ]
    for load in loads:
        load.start()
    barrier = pltpu.get_barrier_semaphore()

    @pl.when(is_relay)
    def _():
        pl.semaphore_signal(barrier, inc=1, device_id=peer, device_id_type=MESH)

    @pl.when(is_owner)
    def _():
        def greet(t, c):
            to = OWNERS - 1 - t
            for q in range(SPLITS):
                ahead = (lax.div(to, 8) == 2) & (lax.rem(to, 2) == 0)

                @pl.when(jnp.logical_not(ahead | ((to == me) & (q == split))))
                def _():
                    pl.semaphore_signal(barrier, inc=1, device_id=(to, q), device_id_type=MESH)
            return c
        lax.fori_loop(0, OWNERS, greet, 0, unroll=UNROLL)

    far_copies = [
        pltpu.make_async_remote_copy(
            src_ref=src, dst_ref=dst, send_sem=give_sem.at[i], recv_sem=got_sem.at[i],
            device_id=peer, device_id_type=MESH,
        )
        for i, (src, dst) in enumerate(((clu_hbm, clu_far), (emb_hbm, emb_far)))
    ]

    @pl.when(is_far)
    def _():
        pl.semaphore_wait(barrier, 1)
        for copy in far_copies:
            copy.start()

    loads[0].wait()
    loads[1].wait()
    cluster = clu_ref[...]
    owner_hot, slot, lane_hot = find_slots(cluster, own_ref[...], lax.rem(here, 16) * CAP)
    loads[2].wait()

    @pl.when(jnp.logical_not(is_far))
    def _():
        fill(emb_ref[...], cluster, owner_hot, slot, lane_hot, send, lab_send)

    @pl.when(jnp.logical_not(is_far))
    def _():
        pl.semaphore_wait(barrier, jnp.where(is_owner, OWNERS - 1, OWNERS))

    first = lax.rem(SPIN_X * split + SPIN_M * me, OWNERS)

    def send_step(o, spot, rows, labels, rows_sem, labels_sem):
        there = home_of(o)
        pltpu.make_async_remote_copy(
            src_ref=labels.at[pl.ds(o, 1)], dst_ref=lab_recv.at[pl.ds(spot, 1)],
            send_sem=labels_sem, recv_sem=lab_sem, device_id=there, device_id_type=MESH,
        ).start()
        pltpu.make_async_remote_copy(
            src_ref=rows.at[o], dst_ref=recv.at[spot],
            send_sem=rows_sem, recv_sem=recv_sem.at[lax.div(spot, 64)], device_id=there, device_id_type=MESH,
        ).start()

    @pl.when(jnp.logical_not(is_far))
    def _():
        def post(t, c):
            o = jnp.where(z >= 2, lax.div(t, 16) * 16 + lax.rem(first + t, 16), lax.rem(first + t, OWNERS))

            @pl.when(jnp.logical_not(is_owner & (o == mine)))
            def _():
                send_step(o, here, send, lab_send, send_sem, lab_send_sem)
            return c
        lax.fori_loop(0, PN, post, 0, unroll=UNROLL)

        @pl.when(is_paced)
        def _():
            wait_bytes(send.at[pl.ds(0, PN)], send_sem)
        lax.fori_loop(PN, OWNERS, post, 0, unroll=UNROLL)

    @pl.when(is_relay)
    def _():
        for copy in far_copies:
            copy.wait_recv()
        cluster = clu_far[...]
        spot = spot_of(3 - z, y, core, split)
        fill(
            emb_far[...], cluster, *find_slots(cluster, own_ref[...], lax.rem(spot, 16) * CAP), send_far, lab_far
        )
        for dx in FAR_DX:
            for dy in FAR_DY:
                for plane in range(2):
                    o = plane * 16 + lax.rem(y + dy, 4) * 4 + lax.rem(split + dx, 4)
                    send_step(o, spot, send_far, lab_far, far_send_sem, lab_far_sem)

    @pl.when(is_owner)
    def _():
        recv[here] = send[mine]
        lab_recv[pl.ds(here, 1)] = lab_send[pl.ds(mine, 1)]
        wait_bytes(lab_recv.at[pl.ds(0, DEVICES - 1)], lab_sem)
        labels = jnp.sum(lab_recv[...].reshape(8, 16, 128), 1)
        eye = iota((ROWS, ROWS), 0) == iota((ROWS, ROWS), 1)
        columns = lax.dot_general(
            eye.astype(jnp.bfloat16), labels.astype(jnp.bfloat16), (((1,), (1,)), ((), ())),
            preferred_element_type=jnp.float32,
        )
        tops, wides = [None] * 8, [None] * 8

        def take(begin, end):
            got = recv[begin // CAP:end // CAP].astype(jnp.float32)
            for h in range(2):
                held[begin:end, h * HALF:(h + 1) * HALF] = (
                    got[:, h * CAP:(h + 1) * CAP].reshape(end - begin, HALF).astype(jnp.bfloat16)
                )

        def score(rows, cols):
            scores = lax.dot_general(
                held[rows[0] * 128:rows[1] * 128, :], held[cols[0] * 128:cols[1] * 128, :],
                (((1,), (1,)), ((), ())), preferred_element_type=jnp.float32,
            )
            for i in range(*rows):
                for j in range(*cols):
                    same = columns[:, i:i + 1] == labels[j:j + 1, :]
                    if i == j:
                        same = same & jnp.logical_not(eye)
                    u, v = (i - rows[0]) * 128, (j - cols[0]) * 128
                    kept = jnp.where(same, scores[u:u + 128, v:v + 128], -2.0)
                    top = jnp.max(kept, 0, keepdims=True)
                    tops[j] = top if tops[j] is None else jnp.maximum(tops[j], top)
                    if not cols[0] <= i < cols[1]:
                        wides[i] = kept if wides[i] is None else jnp.maximum(wides[i], kept)

        def close(i):
            if wides[i] is not None:
                tops[i] = jnp.maximum(tops[i], jnp.max(jnp.transpose(wides[i]), 0, keepdims=True))

        def give(src, m, x):
            @pl.when(jnp.logical_not((m == me) & (x == split)))
            def _():
                pltpu.make_async_remote_copy(
                    src_ref=src, dst_ref=ret_recv.at[pl.ds(mine, 1)],
                    send_sem=ret_send_sem, recv_sem=ret_sem, device_id=(m, x), device_id_type=MESH,
                ).start()

        wait_bytes(recv.at[pl.ds(0, DEVICES // 2 - 1)], recv_sem.at[0])
        take(0, 512)
        wait_bytes(recv.at[pl.ds(0, DEVICES // 2)], recv_sem.at[1])
        take(512, 1024)
        score((0, 2), (0, 2))
        score((0, 4), (2, 4))
        close(0)
        close(1)
        score((4, 8), (0, 2))
        for b in range(2):
            soon[b:b + 1, :] = tops[b]
        for m in (1, 0, 9, 8, 3, 2, 11, 10):
            for x in range(SPLITS):
                give(soon.at[pl.ds(x // 2, 1)], m, x)
        score((4, 8), (2, 4))
        score((4, 6), (4, 6))
        score((4, 8), (6, 8))
        for b in range(4, 6):
            close(b)
        for b in range(6, 8):
            close(b)
        for b in range(8):
            best[b:b + 1, :] = tops[b]

        def give_row(m, c):
            z_to, y_to = lax.div(m, 8), lax.rem(lax.div(m, 2), 4)
            block = lax.div(z_to, 2) * 4 + lax.div(y_to, 2) * 2

            @pl.when(block != 0)
            def _():
                for x in range(SPLITS):
                    give(best.at[pl.ds(block + x // 2, 1)], m, x)
            return c
        lax.fori_loop(0, OWNERS, give_row, 0)
        ret_recv[pl.ds(mine, 1)] = best[pl.ds(lax.div(here, 16), 1)]
        wait_bytes(ret_recv.at[pl.ds(0, OWNERS - 1)], ret_sem)

    @pl.when(jnp.logical_not(is_owner))
    def _():
        wait_bytes(ret_recv, ret_sem)
    rest = ret_recv[...]
    terms = []
    for _ in range(3):
        terms.append(rest.astype(jnp.bfloat16))
        rest = rest - terms[-1].astype(jnp.float32)
    picked = jnp.dot(jnp.concatenate(terms, 0), lane_hot.astype(jnp.bfloat16), preferred_element_type=jnp.float32)
    picked = picked[0:OWNERS] + (picked[OWNERS:2 * OWNERS] + picked[2 * OWNERS:])
    out_ref[...] = jnp.sum(picked * owner_hot, 0, keepdims=True)

    @pl.when(is_owner)
    def _():
        wait_bytes(send.at[pl.ds(0, OWNERS - 1)], send_sem)
        wait_bytes(lab_send.at[pl.ds(0, OWNERS - 1)], lab_send_sem)
        wait_bytes(lab_recv.at[pl.ds(0, DEVICES - 1)], ret_send_sem)

    @pl.when(jnp.logical_not(is_owner | is_far))
    def _():
        @pl.when(is_paced)
        def _():
            wait_bytes(send.at[pl.ds(0, OWNERS - PN)], send_sem)

        @pl.when(jnp.logical_not(is_paced))
        def _():
            wait_bytes(send, send_sem)
        wait_bytes(lab_send, lab_send_sem)

    @pl.when(is_far)
    def _():
        for copy in far_copies:
            copy.wait_send()

    @pl.when(is_relay)
    def _():
        wait_bytes(send_far, far_send_sem)
        wait_bytes(lab_far, lab_far_sem)


def on_device(emb, cluster, owner_of):
    best = pl.pallas_call(
        kernel,
        out_shape=jax.ShapeDtypeStruct((1, ROWS), jnp.float32),
        in_specs=[pl.BlockSpec(memory_space=pltpu.HBM)] * 3,
        out_specs=pl.BlockSpec(memory_space=pltpu.VMEM),
        scratch_shapes=[
            pltpu.VMEM((ROWS, WIDTH), jnp.bfloat16),
            pltpu.VMEM((1, ROWS), jnp.int32),
            pltpu.VMEM((1, CLUSTERS), jnp.int32),
            pltpu.VMEM((OWNERS, 2 * CAP, HALF), jnp.bfloat16),
            pltpu.VMEM((OWNERS, 128), jnp.float32),
            pltpu.VMEM((ROWS, WIDTH), jnp.bfloat16),
            pltpu.VMEM((1, ROWS), jnp.int32),
            pltpu.VMEM((OWNERS, 2 * CAP, HALF), jnp.bfloat16),
            pltpu.VMEM((OWNERS, 128), jnp.float32),
            pltpu.VMEM((DEVICES, 2 * CAP, HALF), jnp.bfloat16),
            pltpu.VMEM((DEVICES, 128), jnp.float32),
            pltpu.VMEM((DEVICES * CAP, WIDTH), jnp.bfloat16),
            pltpu.VMEM((2, 128), jnp.float32),
            pltpu.VMEM((8, 128), jnp.float32),
            pltpu.VMEM((OWNERS, 128), jnp.float32),
            pltpu.SemaphoreType.DMA((3,)),
            pltpu.SemaphoreType.DMA,
            pltpu.SemaphoreType.DMA,
            pltpu.SemaphoreType.DMA,
            pltpu.SemaphoreType.DMA((2,)),
            pltpu.SemaphoreType.DMA,
            pltpu.SemaphoreType.DMA,
            pltpu.SemaphoreType.DMA,
            pltpu.SemaphoreType.DMA,
            pltpu.SemaphoreType.DMA((2,)),
            pltpu.SemaphoreType.DMA((2,)),
        ],
        compiler_params=pltpu.CompilerParams(
            collective_id=0, has_side_effects=True, vmem_limit_bytes=24 * 1024 * 1024
        ),
    )(*[
        pltpu.with_memory_space_constraint(a, pltpu.HBM)
        for a in (emb, cluster.reshape(1, ROWS), owner_of.reshape(1, CLUSTERS))
    ])
    return best.reshape(ROWS)


def solution(mesh):
    return jax.shard_map(
        on_device,
        mesh=mesh,
        in_specs=(P(("owner", "split"), None), P(("owner", "split")), P()),
        out_specs=P(("owner", "split")),
        check_vma=False,
    )
```

```python
import jax
import jax.numpy as jnp
from jax import lax
from jax.experimental import pallas as pl
from jax.experimental.pallas import tpu as pltpu
from jax.sharding import PartitionSpec as P

MESH = pl.DeviceIdType.MESH
OWNERS = 32
SPLITS = 4
CAP = 8
WIDTH = 1024
HALF = WIDTH // 2
ROWS = 128
CLUSTERS = 64
FAR_DX = (2, 1, 3, 0)
FAR_DY = (2, 1, 3, 0)
DEVICES = OWNERS * SPLITS
GROUPS = 4
PER = DEVICES // GROUPS
GROUP_ROWS = PER * CAP
UNROLL = 4
PN = 14
SPIN_X = 5
SPIN_M = 2


def home_of(o):
    return lax.div(o, 4) * 2 + 1, lax.rem(o, 4)


def iota(shape, dim):
    return lax.broadcasted_iota(jnp.int32, shape, dim)


def wait_bytes(ref, sem):
    pltpu.make_async_copy(ref, ref, sem).wait()


def spot_of(z, y, core, x):
    return (
        lax.div(z, 2) * 64 + lax.div(y, 2) * 32 + lax.div(x, 2) * 16
        + lax.rem(y, 2) * 8 + lax.rem(x, 2) * 4 + lax.rem(z, 2) * 2 + core
    )


def find_slots(cluster, owners, lane):
    hot = (iota((CLUSTERS, ROWS), 0) == cluster).astype(jnp.bfloat16)
    table = (iota((OWNERS, CLUSTERS), 0) == owners).astype(jnp.bfloat16)
    owner_hot = jnp.dot(table, hot, preferred_element_type=jnp.float32)
    before = (iota((ROWS, ROWS), 0) < iota((ROWS, ROWS), 1)).astype(jnp.bfloat16)
    count = jnp.dot(owner_hot.astype(jnp.bfloat16), before, preferred_element_type=jnp.float32)
    slot = jnp.sum(
        owner_hot * (count + CAP * iota((OWNERS, ROWS), 0).astype(jnp.float32)), 0, keepdims=True
    ).astype(jnp.int32)
    lane_hot = iota((ROWS, ROWS), 0) == lane + (slot & (CAP - 1))
    return owner_hot, slot, lane_hot


def fill(values, cluster, owner_hot, slot, lane_hot, send, lab_send):
    labels = (owner_hot * (cluster + 1).astype(jnp.float32)).astype(jnp.bfloat16)
    lab_send[...] = lax.dot_general(
        labels, lane_hot.astype(jnp.bfloat16), (((1,), (1,)), ((), ())),
        preferred_element_type=jnp.float32,
    )
    values = values.astype(jnp.float32)
    unit = (values * lax.rsqrt(jnp.sum(values * values, 1, keepdims=True) + 1e-06)).astype(jnp.bfloat16)
    pick = (iota((OWNERS * CAP, ROWS), 0) == slot).astype(jnp.bfloat16)
    parts = [
        jnp.dot(pick, unit[:, h * HALF:(h + 1) * HALF], preferred_element_type=jnp.float32).reshape(
            OWNERS, CAP, HALF
        )
        for h in range(2)
    ]
    send[...] = jnp.concatenate(parts, 1).astype(jnp.bfloat16)


def kernel(
    emb_hbm, clu_hbm, own_hbm, out_ref,
    emb_ref, clu_ref, own_ref, send, lab_send, emb_far, clu_far, send_far, lab_far, recv, lab_recv, held, soon, best, ret_recv,
    load_sem, send_sem, lab_send_sem, ret_send_sem, recv_sem, lab_sem, ret_sem,
    far_send_sem, lab_far_sem, give_sem, got_sem,
):
    me = lax.axis_index("owner")
    split = lax.axis_index("split")
    z, y, core = lax.div(me, 8), lax.rem(lax.div(me, 2), 4), lax.rem(me, 2)
    here = spot_of(z, y, core, split)
    is_far = (z == 2) & (core == 0)
    is_relay = (z == 1) & (core == 0)
    is_paced = (z >= 2) & (core == 1)
    peer = ((3 - z) * 8 + y * 2 + core, split)
    is_owner = (lax.rem(me, 2) == 1) & (me < 16)
    mine = lax.rem(lax.div(me, 2), 8) * 4 + split
    loads = [
        pltpu.make_async_copy(src, dst, load_sem.at[i])
        for i, (src, dst) in enumerate(((clu_hbm, clu_ref), (own_hbm, own_ref), (emb_hbm, emb_ref)))
    ]
    for load in loads:
        load.start()
    barrier = pltpu.get_barrier_semaphore()

    @pl.when(is_relay)
    def _():
        pl.semaphore_signal(barrier, inc=1, device_id=peer, device_id_type=MESH)

    @pl.when(is_owner)
    def _():
        def greet(t, c):
            to = OWNERS - 1 - t
            for q in range(SPLITS):
                ahead = (lax.div(to, 8) == 2) & (lax.rem(to, 2) == 0)

                @pl.when(jnp.logical_not(ahead | ((to == me) & (q == split))))
                def _():
                    pl.semaphore_signal(barrier, inc=1, device_id=(to, q), device_id_type=MESH)
            return c
        lax.fori_loop(0, OWNERS, greet, 0, unroll=UNROLL)

    far_copies = [
        pltpu.make_async_remote_copy(
            src_ref=src, dst_ref=dst, send_sem=give_sem.at[i], recv_sem=got_sem.at[i],
            device_id=peer, device_id_type=MESH,
        )
        for i, (src, dst) in enumerate(((clu_hbm, clu_far), (emb_hbm, emb_far)))
    ]

    @pl.when(is_far)
    def _():
        pl.semaphore_wait(barrier, 1)
        for copy in far_copies:
            copy.start()

    loads[0].wait()
    loads[1].wait()
    cluster = clu_ref[...]
    owner_hot, slot, lane_hot = find_slots(cluster, own_ref[...], lax.rem(here, 16) * CAP)
    loads[2].wait()

    @pl.when(jnp.logical_not(is_far))
    def _():
        fill(emb_ref[...], cluster, owner_hot, slot, lane_hot, send, lab_send)

    @pl.when(jnp.logical_not(is_far))
    def _():
        pl.semaphore_wait(barrier, jnp.where(is_owner, OWNERS - 1, OWNERS))

    first = lax.rem(SPIN_X * split + SPIN_M * me, OWNERS)

    def send_step(o, spot, rows, labels, rows_sem, labels_sem):
        there = home_of(o)
        pltpu.make_async_remote_copy(
            src_ref=labels.at[pl.ds(o, 1)], dst_ref=lab_recv.at[pl.ds(spot, 1)],
            send_sem=labels_sem, recv_sem=lab_sem, device_id=there, device_id_type=MESH,
        ).start()
        pltpu.make_async_remote_copy(
            src_ref=rows.at[o], dst_ref=recv.at[spot],
            send_sem=rows_sem, recv_sem=recv_sem.at[lax.div(spot, 64)], device_id=there, device_id_type=MESH,
        ).start()

    @pl.when(jnp.logical_not(is_far))
    def _():
        def post(t, c):
            o = jnp.where(z >= 2, lax.div(t, 16) * 16 + lax.rem(first + t, 16), lax.rem(first + t, OWNERS))

            @pl.when(jnp.logical_not(is_owner & (o == mine)))
            def _():
                send_step(o, here, send, lab_send, send_sem, lab_send_sem)
            return c
        lax.fori_loop(0, PN, post, 0, unroll=UNROLL)

        @pl.when(is_paced)
        def _():
            wait_bytes(send.at[pl.ds(0, PN)], send_sem)
        lax.fori_loop(PN, OWNERS, post, 0, unroll=UNROLL)

    @pl.when(is_relay)
    def _():
        for copy in far_copies:
            copy.wait_recv()
        cluster = clu_far[...]
        spot = spot_of(3 - z, y, core, split)
        fill(
            emb_far[...], cluster, *find_slots(cluster, own_ref[...], lax.rem(spot, 16) * CAP), send_far, lab_far
        )
        for dx in FAR_DX:
            for dy in FAR_DY:
                for plane in range(2):
                    o = plane * 16 + lax.rem(y + dy, 4) * 4 + lax.rem(split + dx, 4)
                    send_step(o, spot, send_far, lab_far, far_send_sem, lab_far_sem)

    @pl.when(is_owner)
    def _():
        recv[here] = send[mine]
        lab_recv[pl.ds(here, 1)] = lab_send[pl.ds(mine, 1)]
        wait_bytes(lab_recv.at[pl.ds(0, DEVICES - 1)], lab_sem)
        labels = jnp.sum(lab_recv[...].reshape(8, 16, 128), 1)
        eye = iota((ROWS, ROWS), 0) == iota((ROWS, ROWS), 1)
        columns = lax.dot_general(
            eye.astype(jnp.bfloat16), labels.astype(jnp.bfloat16), (((1,), (1,)), ((), ())),
            preferred_element_type=jnp.float32,
        )
        tops, wides = [None] * 8, [None] * 8

        def take(begin, end):
            got = recv[begin // CAP:end // CAP].astype(jnp.float32)
            for h in range(2):
                held[begin:end, h * HALF:(h + 1) * HALF] = (
                    got[:, h * CAP:(h + 1) * CAP].reshape(end - begin, HALF).astype(jnp.bfloat16)
                )

        def score(rows, cols):
            scores = lax.dot_general(
                held[rows[0] * 128:rows[1] * 128, :], held[cols[0] * 128:cols[1] * 128, :],
                (((1,), (1,)), ((), ())), preferred_element_type=jnp.float32,
            )
            for i in range(*rows):
                for j in range(*cols):
                    same = columns[:, i:i + 1] == labels[j:j + 1, :]
                    if i == j:
                        same = same & jnp.logical_not(eye)
                    u, v = (i - rows[0]) * 128, (j - cols[0]) * 128
                    kept = jnp.where(same, scores[u:u + 128, v:v + 128], -2.0)
                    top = jnp.max(kept, 0, keepdims=True)
                    tops[j] = top if tops[j] is None else jnp.maximum(tops[j], top)
                    if not cols[0] <= i < cols[1]:
                        wides[i] = kept if wides[i] is None else jnp.maximum(wides[i], kept)

        def close(i):
            if wides[i] is not None:
                tops[i] = jnp.maximum(tops[i], jnp.max(jnp.transpose(wides[i]), 0, keepdims=True))

        def give(src, m, x):
            @pl.when(jnp.logical_not((m == me) & (x == split)))
            def _():
                pltpu.make_async_remote_copy(
                    src_ref=src, dst_ref=ret_recv.at[pl.ds(mine, 1)],
                    send_sem=ret_send_sem, recv_sem=ret_sem, device_id=(m, x), device_id_type=MESH,
                ).start()

        wait_bytes(recv.at[pl.ds(0, DEVICES // 2 - 1)], recv_sem.at[0])
        take(0, 512)
        wait_bytes(recv.at[pl.ds(0, DEVICES // 2)], recv_sem.at[1])
        take(512, 1024)
        score((0, 2), (0, 2))
        score((0, 4), (2, 4))
        close(0)
        close(1)
        score((4, 8), (0, 2))
        for b in range(2):
            soon[b:b + 1, :] = tops[b]
        for m in (1, 0, 9, 8, 3, 2, 11, 10):
            for x in range(SPLITS):
                give(soon.at[pl.ds(x // 2, 1)], m, x)
        score((4, 8), (2, 4))
        score((4, 6), (4, 6))
        score((4, 8), (6, 8))
        for b in range(4, 6):
            close(b)
        for b in range(6, 8):
            close(b)
        for b in range(8):
            best[b:b + 1, :] = tops[b]

        def give_row(m, c):
            z_to, y_to = lax.div(m, 8), lax.rem(lax.div(m, 2), 4)
            block = lax.div(z_to, 2) * 4 + lax.div(y_to, 2) * 2

            @pl.when(block != 0)
            def _():
                for x in range(SPLITS):
                    give(best.at[pl.ds(block + x // 2, 1)], m, x)
            return c
        lax.fori_loop(0, OWNERS, give_row, 0)
        ret_recv[pl.ds(mine, 1)] = best[pl.ds(lax.div(here, 16), 1)]
        wait_bytes(ret_recv.at[pl.ds(0, OWNERS - 1)], ret_sem)

    @pl.when(jnp.logical_not(is_owner))
    def _():
        wait_bytes(ret_recv, ret_sem)
    rest = ret_recv[...]
    terms = []
    for _ in range(3):
        terms.append(rest.astype(jnp.bfloat16))
        rest = rest - terms[-1].astype(jnp.float32)
    picked = jnp.dot(jnp.concatenate(terms, 0), lane_hot.astype(jnp.bfloat16), preferred_element_type=jnp.float32)
    picked = picked[0:OWNERS] + (picked[OWNERS:2 * OWNERS] + picked[2 * OWNERS:])
    out_ref[...] = jnp.sum(picked * owner_hot, 0, keepdims=True)

    @pl.when(is_owner)
    def _():
        wait_bytes(send.at[pl.ds(0, OWNERS - 1)], send_sem)
        wait_bytes(lab_send.at[pl.ds(0, OWNERS - 1)], lab_send_sem)
        wait_bytes(lab_recv.at[pl.ds(0, DEVICES - 1)], ret_send_sem)

    @pl.when(jnp.logical_not(is_owner | is_far))
    def _():
        @pl.when(is_paced)
        def _():
            wait_bytes(send.at[pl.ds(0, OWNERS - PN)], send_sem)

        @pl.when(jnp.logical_not(is_paced))
        def _():
            wait_bytes(send, send_sem)
        wait_bytes(lab_send, lab_send_sem)

    @pl.when(is_far)
    def _():
        for copy in far_copies:
            copy.wait_send()

    @pl.when(is_relay)
    def _():
        wait_bytes(send_far, far_send_sem)
        wait_bytes(lab_far, lab_far_sem)


def on_device(emb, cluster, owner_of):
    best = pl.pallas_call(
        kernel,
        out_shape=jax.ShapeDtypeStruct((1, ROWS), jnp.float32),
        in_specs=[pl.BlockSpec(memory_space=pltpu.HBM)] * 3,
        out_specs=pl.BlockSpec(memory_space=pltpu.VMEM),
        scratch_shapes=[
            pltpu.VMEM((ROWS, WIDTH), jnp.bfloat16),
            pltpu.VMEM((1, ROWS), jnp.int32),
            pltpu.VMEM((1, CLUSTERS), jnp.int32),
            pltpu.VMEM((OWNERS, 2 * CAP, HALF), jnp.bfloat16),
            pltpu.VMEM((OWNERS, 128), jnp.float32),
            pltpu.VMEM((ROWS, WIDTH), jnp.bfloat16),
            pltpu.VMEM((1, ROWS), jnp.int32),
            pltpu.VMEM((OWNERS, 2 * CAP, HALF), jnp.bfloat16),
            pltpu.VMEM((OWNERS, 128), jnp.float32),
            pltpu.VMEM((DEVICES, 2 * CAP, HALF), jnp.bfloat16),
            pltpu.VMEM((DEVICES, 128), jnp.float32),
            pltpu.VMEM((DEVICES * CAP, WIDTH), jnp.bfloat16),
            pltpu.VMEM((2, 128), jnp.float32),
            pltpu.VMEM((8, 128), jnp.float32),
            pltpu.VMEM((OWNERS, 128), jnp.float32),
            pltpu.SemaphoreType.DMA((3,)),
            pltpu.SemaphoreType.DMA,
            pltpu.SemaphoreType.DMA,
            pltpu.SemaphoreType.DMA,
            pltpu.SemaphoreType.DMA((2,)),
            pltpu.SemaphoreType.DMA,
            pltpu.SemaphoreType.DMA,
            pltpu.SemaphoreType.DMA,
            pltpu.SemaphoreType.DMA,
            pltpu.SemaphoreType.DMA((2,)),
            pltpu.SemaphoreType.DMA((2,)),
        ],
        compiler_params=pltpu.CompilerParams(
            collective_id=0, has_side_effects=True, vmem_limit_bytes=24 * 1024 * 1024
        ),
    )(*[
        pltpu.with_memory_space_constraint(a, pltpu.HBM)
        for a in (emb, cluster.reshape(1, ROWS), owner_of.reshape(1, CLUSTERS))
    ])
    return best.reshape(ROWS)


def solution(mesh):
    return jax.shard_map(
        on_device,
        mesh=mesh,
        in_specs=(P(("owner", "split"), None), P(("owner", "split")), P()),
        out_specs=P(("owner", "split")),
        check_vma=False,
    )
```

```python
import jax
import jax.numpy as jnp
from jax import lax
from jax.experimental import pallas as pl
from jax.experimental.pallas import tpu as pltpu
from jax.sharding import PartitionSpec as P

MESH = pl.DeviceIdType.MESH
OWNERS = 32
SPLITS = 4
CAP = 8
WIDTH = 1024
HALF = WIDTH // 2
ROWS = 128
CLUSTERS = 64
FAR_DX = (2, 1, 3, 0)
FAR_DY = (2, 1, 3, 0)
DEVICES = OWNERS * SPLITS
GROUPS = 4
PER = DEVICES // GROUPS
GROUP_ROWS = PER * CAP
UNROLL = 4
PACES = ((12, 3), (16, 2))
SPIN_X = 5
SPIN_M = 2


def home_of(o):
    return lax.div(o, 4) * 2 + 1, lax.rem(o, 4)


def iota(shape, dim):
    return lax.broadcasted_iota(jnp.int32, shape, dim)


def wait_bytes(ref, sem):
    pltpu.make_async_copy(ref, ref, sem).wait()


def spot_of(z, y, core, x):
    return (
        lax.div(z, 2) * 64 + lax.div(y, 2) * 32 + lax.div(x, 2) * 16
        + lax.rem(y, 2) * 8 + lax.rem(x, 2) * 4 + lax.rem(z, 2) * 2 + core
    )


def find_slots(cluster, owners, lane):
    hot = (iota((CLUSTERS, ROWS), 0) == cluster).astype(jnp.bfloat16)
    table = (iota((OWNERS, CLUSTERS), 0) == owners).astype(jnp.bfloat16)
    owner_hot = jnp.dot(table, hot, preferred_element_type=jnp.float32)
    before = (iota((ROWS, ROWS), 0) < iota((ROWS, ROWS), 1)).astype(jnp.bfloat16)
    count = jnp.dot(owner_hot.astype(jnp.bfloat16), before, preferred_element_type=jnp.float32)
    slot = jnp.sum(
        owner_hot * (count + CAP * iota((OWNERS, ROWS), 0).astype(jnp.float32)), 0, keepdims=True
    ).astype(jnp.int32)
    lane_hot = iota((ROWS, ROWS), 0) == lane + (slot & (CAP - 1))
    return owner_hot, slot, lane_hot


def fill(values, cluster, owner_hot, slot, lane_hot, send, lab_send):
    labels = (owner_hot * (cluster + 1).astype(jnp.float32)).astype(jnp.bfloat16)
    lab_send[...] = lax.dot_general(
        labels, lane_hot.astype(jnp.bfloat16), (((1,), (1,)), ((), ())),
        preferred_element_type=jnp.float32,
    )
    values = values.astype(jnp.float32)
    unit = (values * lax.rsqrt(jnp.sum(values * values, 1, keepdims=True) + 1e-06)).astype(jnp.bfloat16)
    pick = (iota((OWNERS * CAP, ROWS), 0) == slot).astype(jnp.bfloat16)
    parts = [
        jnp.dot(pick, unit[:, h * HALF:(h + 1) * HALF], preferred_element_type=jnp.float32).reshape(
            OWNERS, CAP, HALF
        )
        for h in range(2)
    ]
    send[...] = jnp.concatenate(parts, 1).astype(jnp.bfloat16)


def kernel(
    emb_hbm, clu_hbm, own_hbm, out_ref,
    emb_ref, clu_ref, own_ref, send, lab_send, emb_far, clu_far, send_far, lab_far, recv, lab_recv, held, soon, best, ret_recv,
    load_sem, send_sem, lab_send_sem, ret_send_sem, recv_sem, lab_sem, ret_sem,
    far_send_sem, lab_far_sem, give_sem, got_sem,
):
    me = lax.axis_index("owner")
    split = lax.axis_index("split")
    z, y, core = lax.div(me, 8), lax.rem(lax.div(me, 2), 4), lax.rem(me, 2)
    here = spot_of(z, y, core, split)
    is_far = (z == 2) & (core == 0)
    is_relay = (z == 1) & (core == 0)
    is_paced = (z >= 2) & (core == 1)
    peer = ((3 - z) * 8 + y * 2 + core, split)
    is_owner = (lax.rem(me, 2) == 1) & (me < 16)
    mine = lax.rem(lax.div(me, 2), 8) * 4 + split
    loads = [
        pltpu.make_async_copy(src, dst, load_sem.at[i])
        for i, (src, dst) in enumerate(((clu_hbm, clu_ref), (own_hbm, own_ref), (emb_hbm, emb_ref)))
    ]
    for load in loads:
        load.start()
    barrier = pltpu.get_barrier_semaphore()

    @pl.when(is_relay)
    def _():
        pl.semaphore_signal(barrier, inc=1, device_id=peer, device_id_type=MESH)

    @pl.when(is_owner)
    def _():
        def greet(t, c):
            to = OWNERS - 1 - t
            for q in range(SPLITS):
                ahead = (lax.div(to, 8) == 2) & (lax.rem(to, 2) == 0)

                @pl.when(jnp.logical_not(ahead | ((to == me) & (q == split))))
                def _():
                    pl.semaphore_signal(barrier, inc=1, device_id=(to, q), device_id_type=MESH)
            return c
        lax.fori_loop(0, OWNERS, greet, 0, unroll=UNROLL)

    far_copies = [
        pltpu.make_async_remote_copy(
            src_ref=src, dst_ref=dst, send_sem=give_sem.at[i], recv_sem=got_sem.at[i],
            device_id=peer, device_id_type=MESH,
        )
        for i, (src, dst) in enumerate(((clu_hbm, clu_far), (emb_hbm, emb_far)))
    ]

    @pl.when(is_far)
    def _():
        pl.semaphore_wait(barrier, 1)
        for copy in far_copies:
            copy.start()

    loads[0].wait()
    loads[1].wait()
    cluster = clu_ref[...]
    owner_hot, slot, lane_hot = find_slots(cluster, own_ref[...], lax.rem(here, 16) * CAP)
    loads[2].wait()

    @pl.when(jnp.logical_not(is_far))
    def _():
        fill(emb_ref[...], cluster, owner_hot, slot, lane_hot, send, lab_send)

    @pl.when(jnp.logical_not(is_far))
    def _():
        pl.semaphore_wait(barrier, jnp.where(is_owner, OWNERS - 1, OWNERS))

    first = lax.rem(SPIN_X * split + SPIN_M * me, OWNERS)

    def send_step(o, spot, rows, labels, rows_sem, labels_sem):
        there = home_of(o)
        pltpu.make_async_remote_copy(
            src_ref=labels.at[pl.ds(o, 1)], dst_ref=lab_recv.at[pl.ds(spot, 1)],
            send_sem=labels_sem, recv_sem=lab_sem, device_id=there, device_id_type=MESH,
        ).start()
        pltpu.make_async_remote_copy(
            src_ref=rows.at[o], dst_ref=recv.at[spot],
            send_sem=rows_sem, recv_sem=recv_sem.at[lax.div(spot, 64)], device_id=there, device_id_type=MESH,
        ).start()

    @pl.when(jnp.logical_not(is_far))
    def _():
        def post(t, c):
            o = jnp.where(z >= 2, lax.div(t, 16) * 16 + lax.rem(first + t, 16), lax.rem(first + t, OWNERS))

            @pl.when(jnp.logical_not(is_owner & (o == mine)))
            def _():
                send_step(o, here, send, lab_send, send_sem, lab_send_sem)
            return c
        begin = 0
        for count, plane in PACES:
            lax.fori_loop(begin, count, post, 0, unroll=UNROLL)
            begin = count

            @pl.when(is_paced & (z == plane))
            def _():
                wait_bytes(send.at[pl.ds(0, count)], send_sem)
        lax.fori_loop(begin, OWNERS, post, 0, unroll=UNROLL)

    @pl.when(is_relay)
    def _():
        for copy in far_copies:
            copy.wait_recv()
        cluster = clu_far[...]
        spot = spot_of(3 - z, y, core, split)
        fill(
            emb_far[...], cluster, *find_slots(cluster, own_ref[...], lax.rem(spot, 16) * CAP), send_far, lab_far
        )
        for dx in FAR_DX:
            for dy in FAR_DY:
                for plane in range(2):
                    o = plane * 16 + lax.rem(y + dy, 4) * 4 + lax.rem(split + dx, 4)
                    send_step(o, spot, send_far, lab_far, far_send_sem, lab_far_sem)

    @pl.when(is_owner)
    def _():
        recv[here] = send[mine]
        lab_recv[pl.ds(here, 1)] = lab_send[pl.ds(mine, 1)]
        wait_bytes(lab_recv.at[pl.ds(0, DEVICES - 1)], lab_sem)
        labels = jnp.sum(lab_recv[...].reshape(8, 16, 128), 1)
        eye = iota((ROWS, ROWS), 0) == iota((ROWS, ROWS), 1)
        columns = lax.dot_general(
            eye.astype(jnp.bfloat16), labels.astype(jnp.bfloat16), (((1,), (1,)), ((), ())),
            preferred_element_type=jnp.float32,
        )
        tops, wides = [None] * 8, [None] * 8

        def take(begin, end):
            got = recv[begin // CAP:end // CAP].astype(jnp.float32)
            for h in range(2):
                held[begin:end, h * HALF:(h + 1) * HALF] = (
                    got[:, h * CAP:(h + 1) * CAP].reshape(end - begin, HALF).astype(jnp.bfloat16)
                )

        def score(rows, cols):
            scores = lax.dot_general(
                held[rows[0] * 128:rows[1] * 128, :], held[cols[0] * 128:cols[1] * 128, :],
                (((1,), (1,)), ((), ())), preferred_element_type=jnp.float32,
            )
            for i in range(*rows):
                for j in range(*cols):
                    same = columns[:, i:i + 1] == labels[j:j + 1, :]
                    if i == j:
                        same = same & jnp.logical_not(eye)
                    u, v = (i - rows[0]) * 128, (j - cols[0]) * 128
                    kept = jnp.where(same, scores[u:u + 128, v:v + 128], -2.0)
                    top = jnp.max(kept, 0, keepdims=True)
                    tops[j] = top if tops[j] is None else jnp.maximum(tops[j], top)
                    if not cols[0] <= i < cols[1]:
                        wides[i] = kept if wides[i] is None else jnp.maximum(wides[i], kept)

        def close(i):
            if wides[i] is not None:
                tops[i] = jnp.maximum(tops[i], jnp.max(jnp.transpose(wides[i]), 0, keepdims=True))

        def give(src, m, x):
            @pl.when(jnp.logical_not((m == me) & (x == split)))
            def _():
                pltpu.make_async_remote_copy(
                    src_ref=src, dst_ref=ret_recv.at[pl.ds(mine, 1)],
                    send_sem=ret_send_sem, recv_sem=ret_sem, device_id=(m, x), device_id_type=MESH,
                ).start()

        wait_bytes(recv.at[pl.ds(0, DEVICES // 2 - 1)], recv_sem.at[0])
        take(0, 512)
        wait_bytes(recv.at[pl.ds(0, DEVICES // 2)], recv_sem.at[1])
        take(512, 1024)
        score((0, 2), (0, 2))
        score((0, 4), (2, 4))
        close(0)
        close(1)
        score((4, 8), (0, 2))
        for b in range(2):
            soon[b:b + 1, :] = tops[b]
        for m in (1, 0, 9, 8, 3, 2, 11, 10):
            for x in range(SPLITS):
                give(soon.at[pl.ds(x // 2, 1)], m, x)
        score((4, 8), (2, 4))
        score((4, 6), (4, 6))
        score((4, 8), (6, 8))
        for b in range(4, 6):
            close(b)
        for b in range(6, 8):
            close(b)
        for b in range(8):
            best[b:b + 1, :] = tops[b]

        def give_row(m, c):
            z_to, y_to = lax.div(m, 8), lax.rem(lax.div(m, 2), 4)
            block = lax.div(z_to, 2) * 4 + lax.div(y_to, 2) * 2

            @pl.when(block != 0)
            def _():
                for x in range(SPLITS):
                    give(best.at[pl.ds(block + x // 2, 1)], m, x)
            return c
        lax.fori_loop(0, OWNERS, give_row, 0)
        ret_recv[pl.ds(mine, 1)] = best[pl.ds(lax.div(here, 16), 1)]
        wait_bytes(ret_recv.at[pl.ds(0, OWNERS - 1)], ret_sem)

    @pl.when(jnp.logical_not(is_owner))
    def _():
        wait_bytes(ret_recv, ret_sem)
    rest = ret_recv[...]
    terms = []
    for _ in range(3):
        terms.append(rest.astype(jnp.bfloat16))
        rest = rest - terms[-1].astype(jnp.float32)
    picked = jnp.dot(jnp.concatenate(terms, 0), lane_hot.astype(jnp.bfloat16), preferred_element_type=jnp.float32)
    picked = picked[0:OWNERS] + (picked[OWNERS:2 * OWNERS] + picked[2 * OWNERS:])
    out_ref[...] = jnp.sum(picked * owner_hot, 0, keepdims=True)

    @pl.when(is_owner)
    def _():
        wait_bytes(send.at[pl.ds(0, OWNERS - 1)], send_sem)
        wait_bytes(lab_send.at[pl.ds(0, OWNERS - 1)], lab_send_sem)
        wait_bytes(lab_recv.at[pl.ds(0, DEVICES - 1)], ret_send_sem)

    @pl.when(jnp.logical_not(is_owner | is_far))
    def _():
        for count, plane in PACES:
            @pl.when(is_paced & (z == plane))
            def _():
                wait_bytes(send.at[pl.ds(0, OWNERS - count)], send_sem)

        @pl.when(jnp.logical_not(is_paced))
        def _():
            wait_bytes(send, send_sem)
        wait_bytes(lab_send, lab_send_sem)

    @pl.when(is_far)
    def _():
        for copy in far_copies:
            copy.wait_send()

    @pl.when(is_relay)
    def _():
        wait_bytes(send_far, far_send_sem)
        wait_bytes(lab_far, lab_far_sem)


def on_device(emb, cluster, owner_of):
    best = pl.pallas_call(
        kernel,
        out_shape=jax.ShapeDtypeStruct((1, ROWS), jnp.float32),
        in_specs=[pl.BlockSpec(memory_space=pltpu.HBM)] * 3,
        out_specs=pl.BlockSpec(memory_space=pltpu.VMEM),
        scratch_shapes=[
            pltpu.VMEM((ROWS, WIDTH), jnp.bfloat16),
            pltpu.VMEM((1, ROWS), jnp.int32),
            pltpu.VMEM((1, CLUSTERS), jnp.int32),
            pltpu.VMEM((OWNERS, 2 * CAP, HALF), jnp.bfloat16),
            pltpu.VMEM((OWNERS, 128), jnp.float32),
            pltpu.VMEM((ROWS, WIDTH), jnp.bfloat16),
            pltpu.VMEM((1, ROWS), jnp.int32),
            pltpu.VMEM((OWNERS, 2 * CAP, HALF), jnp.bfloat16),
            pltpu.VMEM((OWNERS, 128), jnp.float32),
            pltpu.VMEM((DEVICES, 2 * CAP, HALF), jnp.bfloat16),
            pltpu.VMEM((DEVICES, 128), jnp.float32),
            pltpu.VMEM((DEVICES * CAP, WIDTH), jnp.bfloat16),
            pltpu.VMEM((2, 128), jnp.float32),
            pltpu.VMEM((8, 128), jnp.float32),
            pltpu.VMEM((OWNERS, 128), jnp.float32),
            pltpu.SemaphoreType.DMA((3,)),
            pltpu.SemaphoreType.DMA,
            pltpu.SemaphoreType.DMA,
            pltpu.SemaphoreType.DMA,
            pltpu.SemaphoreType.DMA((2,)),
            pltpu.SemaphoreType.DMA,
            pltpu.SemaphoreType.DMA,
            pltpu.SemaphoreType.DMA,
            pltpu.SemaphoreType.DMA,
            pltpu.SemaphoreType.DMA((2,)),
            pltpu.SemaphoreType.DMA((2,)),
        ],
        compiler_params=pltpu.CompilerParams(
            collective_id=0, has_side_effects=True, vmem_limit_bytes=24 * 1024 * 1024
        ),
    )(*[
        pltpu.with_memory_space_constraint(a, pltpu.HBM)
        for a in (emb, cluster.reshape(1, ROWS), owner_of.reshape(1, CLUSTERS))
    ])
    return best.reshape(ROWS)


def solution(mesh):
    return jax.shard_map(
        on_device,
        mesh=mesh,
        in_specs=(P(("owner", "split"), None), P(("owner", "split")), P()),
        out_specs=P(("owner", "split")),
        check_vma=False,
    )
```

```python
import jax
import jax.numpy as jnp
from jax import lax
from jax.experimental import pallas as pl
from jax.experimental.pallas import tpu as pltpu
from jax.sharding import PartitionSpec as P

MESH = pl.DeviceIdType.MESH
OWNERS = 32
SPLITS = 4
CAP = 8
WIDTH = 1024
HALF = WIDTH // 2
ROWS = 128
CLUSTERS = 64
FAR_DX = (2, 1, 3, 0)
FAR_DY = (2, 1, 3, 0)
DEVICES = OWNERS * SPLITS
GROUPS = 4
PER = DEVICES // GROUPS
GROUP_ROWS = PER * CAP
UNROLL = 4
PN = 16
SPIN_X = 4
SPIN_M = 8


def home_of(o):
    return lax.div(o, 4) * 2 + 1, lax.rem(o, 4)


def iota(shape, dim):
    return lax.broadcasted_iota(jnp.int32, shape, dim)


def wait_bytes(ref, sem):
    pltpu.make_async_copy(ref, ref, sem).wait()


def spot_of(z, y, core, x):
    return (
        lax.div(z, 2) * 64 + lax.div(y, 2) * 32 + lax.div(x, 2) * 16
        + lax.rem(y, 2) * 8 + lax.rem(x, 2) * 4 + lax.rem(z, 2) * 2 + core
    )


def far_first(i):
    return jnp.where(i == 0, 2, jnp.where(i == 1, 1, jnp.where(i == 2, 3, 0)))


def find_slots(cluster, owners, lane):
    hot = (iota((CLUSTERS, ROWS), 0) == cluster).astype(jnp.bfloat16)
    table = (iota((OWNERS, CLUSTERS), 0) == owners).astype(jnp.bfloat16)
    owner_hot = jnp.dot(table, hot, preferred_element_type=jnp.float32)
    before = (iota((ROWS, ROWS), 0) < iota((ROWS, ROWS), 1)).astype(jnp.bfloat16)
    count = jnp.dot(owner_hot.astype(jnp.bfloat16), before, preferred_element_type=jnp.float32)
    slot = jnp.sum(
        owner_hot * (count + CAP * iota((OWNERS, ROWS), 0).astype(jnp.float32)), 0, keepdims=True
    ).astype(jnp.int32)
    lane_hot = iota((ROWS, ROWS), 0) == lane + (slot & (CAP - 1))
    return owner_hot, slot, lane_hot


def fill(values, cluster, owner_hot, slot, lane_hot, send, lab_send):
    labels = (owner_hot * (cluster + 1).astype(jnp.float32)).astype(jnp.bfloat16)
    lab_send[...] = lax.dot_general(
        labels, lane_hot.astype(jnp.bfloat16), (((1,), (1,)), ((), ())),
        preferred_element_type=jnp.float32,
    )
    values = values.astype(jnp.float32)
    unit = (values * lax.rsqrt(jnp.sum(values * values, 1, keepdims=True) + 1e-06)).astype(jnp.bfloat16)
    pick = (iota((OWNERS * CAP, ROWS), 0) == slot).astype(jnp.bfloat16)
    parts = [
        jnp.dot(pick, unit[:, h * HALF:(h + 1) * HALF], preferred_element_type=jnp.float32).reshape(
            OWNERS, CAP, HALF
        )
        for h in range(2)
    ]
    send[...] = jnp.concatenate(parts, 1).astype(jnp.bfloat16)


def kernel(
    emb_hbm, clu_hbm, own_hbm, out_ref,
    emb_ref, clu_ref, own_ref, send, lab_send, emb_far, clu_far, send_far, lab_far, recv, lab_recv, held, soon, best, ret_recv,
    load_sem, send_sem, lab_send_sem, ret_send_sem, recv_sem, lab_sem, ret_sem,
    far_send_sem, lab_far_sem, give_sem, got_sem,
):
    me = lax.axis_index("owner")
    split = lax.axis_index("split")
    z, y, core = lax.div(me, 8), lax.rem(lax.div(me, 2), 4), lax.rem(me, 2)
    here = spot_of(z, y, core, split)
    is_far = (z == 2) & (core == 0)
    is_relay = (z == 1) & (core == 0)
    is_paced = (z >= 2) & (core == 1)
    peer = ((3 - z) * 8 + y * 2 + core, split)
    is_owner = (lax.rem(me, 2) == 1) & (me < 16)
    mine = lax.rem(lax.div(me, 2), 8) * 4 + split
    loads = [
        pltpu.make_async_copy(src, dst, load_sem.at[i])
        for i, (src, dst) in enumerate(((clu_hbm, clu_ref), (own_hbm, own_ref), (emb_hbm, emb_ref)))
    ]
    for load in loads:
        load.start()
    barrier = pltpu.get_barrier_semaphore()

    @pl.when(is_relay)
    def _():
        pl.semaphore_signal(barrier, inc=1, device_id=peer, device_id_type=MESH)

    @pl.when(is_owner)
    def _():
        def greet(t, c):
            to = OWNERS - 1 - t
            for q in range(SPLITS):
                ahead = (lax.div(to, 8) == 2) & (lax.rem(to, 2) == 0)

                @pl.when(jnp.logical_not(ahead | ((to == me) & (q == split))))
                def _():
                    pl.semaphore_signal(barrier, inc=1, device_id=(to, q), device_id_type=MESH)
            return c
        lax.fori_loop(0, OWNERS, greet, 0, unroll=UNROLL)

    far_copies = [
        pltpu.make_async_remote_copy(
            src_ref=src, dst_ref=dst, send_sem=give_sem.at[i], recv_sem=got_sem.at[i],
            device_id=peer, device_id_type=MESH,
        )
        for i, (src, dst) in enumerate(((clu_hbm, clu_far), (emb_hbm, emb_far)))
    ]

    @pl.when(is_far)
    def _():
        pl.semaphore_wait(barrier, 1)
        for copy in far_copies:
            copy.start()

    loads[0].wait()
    loads[1].wait()
    cluster = clu_ref[...]
    owner_hot, slot, lane_hot = find_slots(cluster, own_ref[...], lax.rem(here, 16) * CAP)
    loads[2].wait()

    @pl.when(jnp.logical_not(is_far))
    def _():
        fill(emb_ref[...], cluster, owner_hot, slot, lane_hot, send, lab_send)

    @pl.when(jnp.logical_not(is_far))
    def _():
        pl.semaphore_wait(barrier, jnp.where(is_owner, OWNERS - 1, OWNERS))

    first = lax.rem(SPIN_X * split + SPIN_M * me, OWNERS)

    def send_step(o, spot, rows, labels, rows_sem, labels_sem):
        there = home_of(o)
        pltpu.make_async_remote_copy(
            src_ref=labels.at[pl.ds(o, 1)], dst_ref=lab_recv.at[pl.ds(spot, 1)],
            send_sem=labels_sem, recv_sem=lab_sem, device_id=there, device_id_type=MESH,
        ).start()
        pltpu.make_async_remote_copy(
            src_ref=rows.at[o], dst_ref=recv.at[spot],
            send_sem=rows_sem, recv_sem=recv_sem.at[lax.div(spot, 64)], device_id=there, device_id_type=MESH,
        ).start()

    @pl.when(jnp.logical_not(is_far))
    def _():
        def post(t, c):
            at = jnp.where(z >= 2, lax.rem(t, 16), lax.div(t, 2))
            to_plane = jnp.where(z >= 2, lax.div(t, 16), lax.rem(t, 2))
            dx, dy = far_first(lax.div(at, 4)), far_first(lax.rem(at, 4))
            ordered = to_plane * 16 + lax.rem(y + dy, 4) * 4 + lax.rem(split + dx, 4)
            o = jnp.where(z >= 2, to_plane * 16 + lax.rem(first + t, 16), ordered)

            @pl.when(jnp.logical_not(is_owner & (o == mine)))
            def _():
                send_step(o, here, send, lab_send, send_sem, lab_send_sem)
            return c
        lax.fori_loop(0, PN, post, 0, unroll=UNROLL)

        @pl.when(is_paced)
        def _():
            wait_bytes(send.at[pl.ds(0, PN)], send_sem)
        lax.fori_loop(PN, OWNERS, post, 0, unroll=UNROLL)

    @pl.when(is_relay)
    def _():
        for copy in far_copies:
            copy.wait_recv()
        cluster = clu_far[...]
        spot = spot_of(3 - z, y, core, split)
        fill(
            emb_far[...], cluster, *find_slots(cluster, own_ref[...], lax.rem(spot, 16) * CAP), send_far, lab_far
        )
        for dx in FAR_DX:
            for dy in FAR_DY:
                for plane in range(2):
                    o = plane * 16 + lax.rem(y + dy, 4) * 4 + lax.rem(split + dx, 4)
                    send_step(o, spot, send_far, lab_far, far_send_sem, lab_far_sem)

    @pl.when(is_owner)
    def _():
        recv[here] = send[mine]
        lab_recv[pl.ds(here, 1)] = lab_send[pl.ds(mine, 1)]
        wait_bytes(lab_recv.at[pl.ds(0, DEVICES - 1)], lab_sem)
        labels = jnp.sum(lab_recv[...].reshape(8, 16, 128), 1)
        eye = iota((ROWS, ROWS), 0) == iota((ROWS, ROWS), 1)
        columns = lax.dot_general(
            eye.astype(jnp.bfloat16), labels.astype(jnp.bfloat16), (((1,), (1,)), ((), ())),
            preferred_element_type=jnp.float32,
        )
        tops, wides = [None] * 8, [None] * 8

        def take(begin, end):
            got = recv[begin // CAP:end // CAP].astype(jnp.float32)
            for h in range(2):
                held[begin:end, h * HALF:(h + 1) * HALF] = (
                    got[:, h * CAP:(h + 1) * CAP].reshape(end - begin, HALF).astype(jnp.bfloat16)
                )

        def score(rows, cols):
            scores = lax.dot_general(
                held[rows[0] * 128:rows[1] * 128, :], held[cols[0] * 128:cols[1] * 128, :],
                (((1,), (1,)), ((), ())), preferred_element_type=jnp.float32,
            )
            for i in range(*rows):
                for j in range(*cols):
                    same = columns[:, i:i + 1] == labels[j:j + 1, :]
                    if i == j:
                        same = same & jnp.logical_not(eye)
                    u, v = (i - rows[0]) * 128, (j - cols[0]) * 128
                    kept = jnp.where(same, scores[u:u + 128, v:v + 128], -2.0)
                    top = jnp.max(kept, 0, keepdims=True)
                    tops[j] = top if tops[j] is None else jnp.maximum(tops[j], top)
                    if not cols[0] <= i < cols[1]:
                        wides[i] = kept if wides[i] is None else jnp.maximum(wides[i], kept)

        def close(i):
            if wides[i] is not None:
                tops[i] = jnp.maximum(tops[i], jnp.max(jnp.transpose(wides[i]), 0, keepdims=True))

        def give(src, m, x):
            @pl.when(jnp.logical_not((m == me) & (x == split)))
            def _():
                pltpu.make_async_remote_copy(
                    src_ref=src, dst_ref=ret_recv.at[pl.ds(mine, 1)],
                    send_sem=ret_send_sem, recv_sem=ret_sem, device_id=(m, x), device_id_type=MESH,
                ).start()

        wait_bytes(recv.at[pl.ds(0, DEVICES // 2 - 1)], recv_sem.at[0])
        take(0, 512)
        wait_bytes(recv.at[pl.ds(0, DEVICES // 2)], recv_sem.at[1])
        take(512, 1024)
        score((0, 2), (0, 2))
        score((0, 4), (2, 4))
        close(0)
        close(1)
        score((4, 8), (0, 2))
        for b in range(2):
            soon[b:b + 1, :] = tops[b]
        for m in (1, 0, 9, 8, 3, 2, 11, 10):
            for x in range(SPLITS):
                give(soon.at[pl.ds(x // 2, 1)], m, x)
        score((4, 8), (2, 4))
        score((4, 6), (4, 6))
        score((4, 8), (6, 8))
        for b in range(4, 6):
            close(b)
        for b in range(6, 8):
            close(b)
        for b in range(8):
            best[b:b + 1, :] = tops[b]

        def give_row(m, c):
            z_to, y_to = lax.div(m, 8), lax.rem(lax.div(m, 2), 4)
            block = lax.div(z_to, 2) * 4 + lax.div(y_to, 2) * 2

            @pl.when(block != 0)
            def _():
                for x in range(SPLITS):
                    give(best.at[pl.ds(block + x // 2, 1)], m, x)
            return c
        lax.fori_loop(0, OWNERS, give_row, 0)
        ret_recv[pl.ds(mine, 1)] = best[pl.ds(lax.div(here, 16), 1)]
        wait_bytes(ret_recv.at[pl.ds(0, OWNERS - 1)], ret_sem)

    @pl.when(jnp.logical_not(is_owner))
    def _():
        wait_bytes(ret_recv, ret_sem)
    rest = ret_recv[...]
    terms = []
    for _ in range(3):
        terms.append(rest.astype(jnp.bfloat16))
        rest = rest - terms[-1].astype(jnp.float32)
    picked = jnp.dot(jnp.concatenate(terms, 0), lane_hot.astype(jnp.bfloat16), preferred_element_type=jnp.float32)
    picked = picked[0:OWNERS] + (picked[OWNERS:2 * OWNERS] + picked[2 * OWNERS:])
    out_ref[...] = jnp.sum(picked * owner_hot, 0, keepdims=True)

    @pl.when(is_owner)
    def _():
        wait_bytes(send.at[pl.ds(0, OWNERS - 1)], send_sem)
        wait_bytes(lab_send.at[pl.ds(0, OWNERS - 1)], lab_send_sem)
        wait_bytes(lab_recv.at[pl.ds(0, DEVICES - 1)], ret_send_sem)

    @pl.when(jnp.logical_not(is_owner | is_far))
    def _():
        @pl.when(is_paced)
        def _():
            wait_bytes(send.at[pl.ds(0, OWNERS - PN)], send_sem)

        @pl.when(jnp.logical_not(is_paced))
        def _():
            wait_bytes(send, send_sem)
        wait_bytes(lab_send, lab_send_sem)

    @pl.when(is_far)
    def _():
        for copy in far_copies:
            copy.wait_send()

    @pl.when(is_relay)
    def _():
        wait_bytes(send_far, far_send_sem)
        wait_bytes(lab_far, lab_far_sem)


def on_device(emb, cluster, owner_of):
    best = pl.pallas_call(
        kernel,
        out_shape=jax.ShapeDtypeStruct((1, ROWS), jnp.float32),
        in_specs=[pl.BlockSpec(memory_space=pltpu.HBM)] * 3,
        out_specs=pl.BlockSpec(memory_space=pltpu.VMEM),
        scratch_shapes=[
            pltpu.VMEM((ROWS, WIDTH), jnp.bfloat16),
            pltpu.VMEM((1, ROWS), jnp.int32),
            pltpu.VMEM((1, CLUSTERS), jnp.int32),
            pltpu.VMEM((OWNERS, 2 * CAP, HALF), jnp.bfloat16),
            pltpu.VMEM((OWNERS, 128), jnp.float32),
            pltpu.VMEM((ROWS, WIDTH), jnp.bfloat16),
            pltpu.VMEM((1, ROWS), jnp.int32),
            pltpu.VMEM((OWNERS, 2 * CAP, HALF), jnp.bfloat16),
            pltpu.VMEM((OWNERS, 128), jnp.float32),
            pltpu.VMEM((DEVICES, 2 * CAP, HALF), jnp.bfloat16),
            pltpu.VMEM((DEVICES, 128), jnp.float32),
            pltpu.VMEM((DEVICES * CAP, WIDTH), jnp.bfloat16),
            pltpu.VMEM((2, 128), jnp.float32),
            pltpu.VMEM((8, 128), jnp.float32),
            pltpu.VMEM((OWNERS, 128), jnp.float32),
            pltpu.SemaphoreType.DMA((3,)),
            pltpu.SemaphoreType.DMA,
            pltpu.SemaphoreType.DMA,
            pltpu.SemaphoreType.DMA,
            pltpu.SemaphoreType.DMA((2,)),
            pltpu.SemaphoreType.DMA,
            pltpu.SemaphoreType.DMA,
            pltpu.SemaphoreType.DMA,
            pltpu.SemaphoreType.DMA,
            pltpu.SemaphoreType.DMA((2,)),
            pltpu.SemaphoreType.DMA((2,)),
        ],
        compiler_params=pltpu.CompilerParams(
            collective_id=0, has_side_effects=True, vmem_limit_bytes=24 * 1024 * 1024
        ),
    )(*[
        pltpu.with_memory_space_constraint(a, pltpu.HBM)
        for a in (emb, cluster.reshape(1, ROWS), owner_of.reshape(1, CLUSTERS))
    ])
    return best.reshape(ROWS)


def solution(mesh):
    return jax.shard_map(
        on_device,
        mesh=mesh,
        in_specs=(P(("owner", "split"), None), P(("owner", "split")), P()),
        out_specs=P(("owner", "split")),
        check_vma=False,
    )
```
